128 devices in a mesh: grp: 8 (over z, core), ep: 16 (over x, y).
Axes of the slice: x: 4, y: 4, z: 4, core: 2. Of those that a mesh axis runs over, the one named last changes fastest.
Arguments:
- tokens: bfloat16 [4096, 7168], P('ep'), may hold values from -6 to 6
- cotangent: bfloat16 [4096, 7168], P('ep'), may hold values from -6 to 6
- expert_ids: int32 [4096, 8], P('ep'), may hold values from 0 to 255, as said below
- gate_scores: float32 [4096, 8], P('ep'), may hold values from 0.1 to 1
- gate_weight: bfloat16 [16, 7168, 1024], P('ep', None, 'grp'), may hold values from -0.0625 to 0.0625
- up_weight: bfloat16 [16, 7168, 1024], P('ep', None, 'grp'), may hold values from -0.0625 to 0.0625
- down_weight: bfloat16 [16, 1024, 7168], P('ep', 'grp'), may hold values from -0.1875 to 0.1875
Outputs:
- grad_tokens: bfloat16 [4096, 7168], P('ep')
- grad_gate_weight: bfloat16 [16, 7168, 1024], P('ep', None, 'grp')
- grad_up_weight: bfloat16 [16, 7168, 1024], P('ep', None, 'grp')
- grad_down_weight: bfloat16 [16, 1024, 7168], P('ep', 'grp')
The draws below stay inside these ranges and needn't reach their ends.
Inputs may be any that keep to these rules, and one draw needn't show every extreme that they name: `expert_ids`: the 8 numbers of a row differ; a row names at most one number below 16; among the 256 rows of one index of ep (aligned blocks), at most 24 name the same number below 16.
All inputs are finite; a program needn't handle non-finite values.
Results may differ from the reference program's by a relative error of at most 0.0057.
Values may be sent and summed in bfloat16 or wider, within the bound.
A program may use at most 128 MiB of HBM per device.

```python
import jax
import jax.numpy as jnp
from jax import lax

D = 7168
EXPERTS = 256
TOPK = 8
HID = 1024
TOK_DEV = 256
MOST = 24
WIN = 16
TOKENS = 4096
N_EP = 16


def draw_expert_ids(key, part):
    key = jax.random.fold_in(key, 11)
    key_hot, key_blocks = jax.random.split(key)
    hot_pair = jax.random.permutation(key_hot, WIN)[:2]
    stride = (EXPERTS - WIN) // TOPK

    def one_block(block_key):
        key_counts, key_second, key_rows, key_offset, key_place = jax.random.split(block_key, 5)
        counts = jax.random.randint(key_counts, (WIN,), 0, MOST // 2 + 1)
        second = jax.random.randint(key_second, (), MOST // 2, MOST + 1)
        counts = counts.at[hot_pair[0]].set(MOST).at[hot_pair[1]].set(second)
        bounds = jnp.cumsum(counts)
        position = jnp.arange(TOK_DEV)
        owner_id = jnp.sum((position[:, None] >= bounds[None, :]).astype(jnp.int32), axis=1)
        owner_id = owner_id[jax.random.permutation(key_rows, TOK_DEV)]
        offset = jax.random.randint(key_offset, (TOK_DEV, 1), 0, EXPERTS - WIN)
        others = WIN + (offset + stride * jnp.arange(TOPK)[None, :]) % (EXPERTS - WIN)
        place_col = jax.random.randint(key_place, (TOK_DEV, 1), 0, TOPK)
        chosen = (jnp.arange(TOPK)[None, :] == place_col) & (owner_id[:, None] < WIN)
        return jnp.where(chosen, owner_id[:, None], others)
    block_keys = jax.random.split(key_blocks, N_EP)
    return jax.vmap(one_block)(block_keys).reshape(TOKENS, TOPK).astype(jnp.int32)


def block_levels(own_key, shape, shards, low, top_value):
    def one(dim, parts):
        steps = jax.random.uniform(jax.random.fold_in(jax.random.fold_in(own_key, 6), dim), (parts,), jnp.float32, low / len(shards), top_value / len(shards))
        return jnp.repeat(jnp.exp(steps), shape[dim] // parts).reshape((-1,) + (1,) * (len(shape) - dim - 1))

    loudness = one(*shards[0])
    for cut in shards[1:]:
        loudness = loudness * one(*cut)
    return loudness


def gaussian(rng, extent, deviation, limit, pieces=(), kind=jnp.bfloat16):
    factor_of = block_levels(rng, extent, pieces, -0.22, 0.18) if pieces else 1.0
    entries = jax.random.normal(rng, extent, jnp.float32) * deviation * factor_of
    return jnp.minimum(jnp.maximum(entries, -limit), limit).astype(kind)


def setup_inputs(seed: int = 0) -> dict:
    streams_of = jax.random.split(jax.random.key(seed), 8)
    tokens = gaussian(streams_of[0], (TOKENS, D), 1.0, 6.0, ((0, 16),))
    cotangent = gaussian(streams_of[1], (TOKENS, D), 1.0, 6.0, ((0, 16),))
    expert_ids = draw_expert_ids(jax.random.fold_in(streams_of[7], 71), 0)
    gate_scores = jnp.clip(0.1 + 0.9 * jax.random.uniform(streams_of[3], (TOKENS, TOPK), jnp.float32) ** block_levels(streams_of[3], (TOKENS, TOPK), ((0, 16),), -0.2, 0.2), 0.1, 1.0)
    gate_weight = gaussian(streams_of[4], (WIN, D, HID), D ** -0.5, 0.0625, ((0, 16), (2, 8)))
    up_weight = gaussian(streams_of[5], (WIN, D, HID), D ** -0.5, 0.0625, ((0, 16), (2, 8)))
    down_weight = gaussian(streams_of[6], (WIN, HID, D), HID ** -0.5, 0.1875, ((0, 16), (1, 8)))
    return dict(tokens=tokens, cotangent=cotangent, expert_ids=expert_ids, gate_scores=gate_scores, gate_weight=gate_weight, up_weight=up_weight, down_weight=down_weight)


def block_slots(block_ids, block_gates):
    row_count = block_ids.shape[0]
    flat_ids = block_ids.reshape(-1)
    occupied = flat_ids < WIN
    onehot = (flat_ids[:, None] == jnp.arange(WIN, dtype=jnp.int32)[None, :]).astype(jnp.int32)
    before = jnp.cumsum(onehot, axis=0) - onehot
    slot_rank = jnp.sum(before * onehot, axis=1).astype(jnp.int32)
    destination = jnp.where(occupied, flat_ids * MOST + slot_rank, WIN * MOST).astype(jnp.int32)
    pair_token = (jnp.arange(flat_ids.shape[0], dtype=jnp.int32) // block_ids.shape[1]).astype(jnp.int32)
    slot_token = jnp.full((WIN * MOST + 1,), row_count, jnp.int32).at[destination].set(pair_token)[:WIN * MOST]
    slot_gate = jnp.zeros((WIN * MOST + 1,), jnp.float32).at[destination].set(block_gates.reshape(-1))[:WIN * MOST]
    return slot_token, slot_gate


def backward_rows(rows_x, rows_c, gate_w, up_w, down_w):
    gate_pre = jnp.dot(rows_x, gate_w, preferred_element_type=jnp.float32)
    up_pre = jnp.dot(rows_x, up_w, preferred_element_type=jnp.float32)
    sigmoid_gate = jax.nn.sigmoid(gate_pre)
    activated = gate_pre * sigmoid_gate
    hidden = (activated * up_pre).astype(jnp.bfloat16)
    grad_hidden = jnp.dot(rows_c, down_w.T, preferred_element_type=jnp.float32)
    grad_up = (grad_hidden * activated).astype(jnp.bfloat16)
    grad_gate = (grad_hidden * up_pre * sigmoid_gate * (1.0 + gate_pre * (1.0 - sigmoid_gate))).astype(jnp.bfloat16)
    down_grad = jnp.dot(hidden.T, rows_c, preferred_element_type=jnp.float32)
    gate_grad = jnp.dot(rows_x.T, grad_gate, preferred_element_type=jnp.float32)
    up_grad = jnp.dot(rows_x.T, grad_up, preferred_element_type=jnp.float32)
    row_grad = jnp.dot(grad_gate, gate_w.T, preferred_element_type=jnp.float32) + jnp.dot(grad_up, up_w.T, preferred_element_type=jnp.float32)
    return gate_grad, up_grad, down_grad, row_grad


def reference(tokens, cotangent, expert_ids, gate_scores, gate_weight, up_weight, down_weight):
    source_ids = expert_ids.reshape(N_EP, TOK_DEV, TOPK)
    source_gates = gate_scores.reshape(N_EP, TOK_DEV, TOPK)
    slot_token, slot_gate = jax.vmap(block_slots)(source_ids, source_gates)
    offsets = (jnp.arange(N_EP, dtype=jnp.int32) * TOK_DEV)[:, None]
    global_token = jnp.where(slot_token < TOK_DEV, slot_token + offsets, TOKENS).astype(jnp.int32)
    per_expert = global_token.reshape(N_EP, WIN, MOST).transpose(1, 0, 2).reshape(WIN, N_EP * MOST)
    per_gate = slot_gate.reshape(N_EP, WIN, MOST).transpose(1, 0, 2).reshape(WIN, N_EP * MOST)
    pad_tokens = jnp.concatenate([tokens, jnp.zeros((1, D), tokens.dtype)], axis=0)
    pad_cotangent = jnp.concatenate([cotangent, jnp.zeros((1, D), cotangent.dtype)], axis=0)

    def one_expert(inputs):
        index_rows, gate_rows, gate_w, up_w, down_w = inputs
        rows_x = pad_tokens[index_rows]
        rows_c = (gate_rows[:, None] * pad_cotangent[index_rows].astype(jnp.float32)).astype(jnp.bfloat16)
        gate_grad, up_grad, down_grad, row_grad = backward_rows(rows_x, rows_c, gate_w, up_w, down_w)
        return (gate_grad.astype(jnp.bfloat16), up_grad.astype(jnp.bfloat16), down_grad.astype(jnp.bfloat16), row_grad.astype(jnp.bfloat16))

    results = lax.map(one_expert, (per_expert, per_gate, gate_weight, up_weight, down_weight))
    rows_back = results[3].reshape(-1, D).astype(jnp.float32)
    grad_tokens = jnp.zeros((TOKENS + 1, D), jnp.float32).at[per_expert.reshape(-1)].add(rows_back)[:TOKENS].astype(jnp.bfloat16)
    return grad_tokens, results[0], results[1], results[2]
```

```python
import functools

import jax
import jax.numpy as jnp
from jax import lax
from jax.experimental import pallas as pl
from jax.experimental.pallas import tpu as pltpu
from jax.sharding import PartitionSpec as P

BF = jnp.bfloat16
F32 = jnp.float32
MESH = pl.DeviceIdType.MESH

N = 16
SIDE = 4
T = 256
HID = 128
D = 7168
H = D // 2
W = 512
U = W // 2
NU = H // W
NG = 4
ND = NU - NG
R16 = N * 16
R8 = N * 8
R = R16 + R8
BLK = 48


def mm(a, b, ca=1, cb=0):
    return lax.dot_general(a, b, (((ca,), (cb,)), ((), ())), preferred_element_type=F32)


def pack(dst, g):
    g16 = g[:R16].reshape(N, 16, W)
    dst[:, 0:16, :] = g16[:, :, :U].astype(BF)
    dst[:, 16:32, :] = g16[:, :, U:].astype(BF)
    g8 = g[R16:].reshape(N, 8, W)
    dst[:, 32:48, :] = jnp.concatenate([g8[:, :, :U], g8[:, :, U:]], axis=1).astype(BF)


def body(
    tok, cot, ids, gs, gw, uw, dw,
    o_tok, o_gate, o_up, o_down,
    tokv, pm, q16, q8a, q8b, gate_col,
    send_a, recv_a, xm, wgu, wd, acc_gu, acc_h, accr_gu, accr_h, hid, g2,
    send_c, recv_c, zp, zr1, zs, zk, zr2, fin, dwgu, dwd,
    tok_sem, w_sem, ws_sem, wr_sem, as_sem, ar_sem, z1s_sem, z1r_sem, z2s_sem, z2r_sem,
    bs_sem, br_sem, cs_sem, cr_sem,
    s1s_sem, s1r_sem, s2s_sem, s2r_sem, g1s_sem, g1r_sem, g2s_sem, g2r_sem,
    ol_sem, os_sem, or_sem, dl_sem, ds_sem, dr_sem,
):
    g = lax.axis_index("grp")
    e = lax.axis_index("ep")
    z, c = g // 2, g % 2
    x, y = e // SIDE, e % SIDE
    other = 1 - c
    za = z + 1 - 2 * (z % 2)
    zb = 3 - z
    zo = 3 - za
    first = (za, zb)
    second = (zb, za)
    sib = (2 * z + other, e)

    def at_z(zz):
        return (2 * zz + c, e)

    def peer(k):
        return ((x + k // SIDE) % SIDE) * SIDE + (y + k % SIDE) % SIDE

    def remote(src, dst, ss, rs, dev):
        return pltpu.make_async_remote_copy(
            src_ref=src, dst_ref=dst, send_sem=ss, recv_sem=rs, device_id=dev, device_id_type=MESH
        )

    def mult(v, m):
        return pl.multiple_of(v, m)

    def unit_of(l):
        return z if l == 0 else NG + l - 1

    def load(a, l):
        src = (tok, cot)[a]
        return pltpu.make_async_copy(
            src.at[:, pl.ds(mult(c * H + unit_of(l) * W, W), W)], tokv.at[a, l], tok_sem.at[a, l]
        )

    for l in range(1 + ND):
        for a in range(2):
            load(a, l).start()

    my_half = mult(c * H, H)
    own_w = [
        pltpu.make_async_copy(gw.at[0, pl.ds(my_half, H)], wgu.at[c], w_sem.at[0]),
        pltpu.make_async_copy(uw.at[0, pl.ds(my_half, H)], wgu.at[2 + c], w_sem.at[1]),
        pltpu.make_async_copy(
            dw.at[0, :, pl.ds(my_half, H)], wd.at[pl.ds(mult(c * HID, HID), HID)], w_sem.at[2]
        ),
    ]
    for cp in own_w:
        cp.start()

    bar = pltpu.get_barrier_semaphore()

    def greet(k, carry):
        pl.semaphore_signal(bar, inc=1, device_id=(g, peer(k)), device_id_type=MESH)
        return carry

    lax.fori_loop(1, N, greet, 0)
    for dev in (at_z(za), at_z(zb), sib):
        pl.semaphore_signal(bar, inc=1, device_id=dev, device_id_type=MESH)

    idf = ids[...].astype(F32)
    e_col = jnp.min(idf, axis=1, keepdims=True)
    e_row = jnp.transpose(jnp.broadcast_to(e_col, (T, 128)))[0:1, :]
    gate_col[...] = jnp.sum(jnp.where(idf < N, gs[...], 0.0), axis=1, keepdims=True)
    sub = lax.broadcasted_iota(jnp.int32, (T, T), 0)
    lane = lax.broadcasted_iota(jnp.int32, (T, T), 1)
    same = e_col == e_row
    rank_row = jnp.sum(jnp.where(same & (sub < lane), 1.0, 0.0), axis=0, keepdims=True)
    rank_col = jnp.sum(jnp.where(same & (lane < sub), 1.0, 0.0), axis=1, keepdims=True)

    def onehot(test):
        return jnp.where(test, 1.0, 0.0).astype(BF)

    sf = lax.broadcasted_iota(jnp.int32, (R16, T), 0)
    pm[:R16, :] = onehot(((sf // 16).astype(F32) == e_row) & ((sf % 16).astype(F32) == rank_row))
    s8 = lax.broadcasted_iota(jnp.int32, (R8, T), 0)
    pm[R16:, :] = onehot(((s8 // 8).astype(F32) == e_row) & ((s8 % 8 + 16).astype(F32) == rank_row))
    of_e = (lane // 16).astype(F32) == e_col
    j16 = lane % 16
    q16[...] = onehot(of_e & (j16.astype(F32) == rank_col))
    late = of_e & ((j16 % 8 + 16).astype(F32) == rank_col)
    q8a[...] = onehot(late & (j16 < 8))
    q8b[...] = onehot(late & (j16 >= 8))

    pl.semaphore_wait(bar, N - 1 + 3)

    their_half = mult(other * H, H)
    sib_w = [
        remote(gw.at[0, pl.ds(their_half, H)], wgu.at[c], ws_sem.at[0], wr_sem.at[0], sib),
        remote(uw.at[0, pl.ds(their_half, H)], wgu.at[2 + c], ws_sem.at[1], wr_sem.at[1], sib),
        remote(
            dw.at[0, :, pl.ds(their_half, H)],
            wd.at[pl.ds(mult(c * HID, HID), HID)],
            ws_sem.at[2], wr_sem.at[2], sib,
        ),
    ]

    for l in range(1 + ND):
        for a in range(2):
            load(a, l).wait()
            u = unit_of(l)
            src = tokv[a, l]
            if a == 1:
                src = (gate_col[...] * src.astype(F32)).astype(BF)
            pack(send_a.at[a, l], mm(pm[...], src))
            recv_a[a, u, e] = send_a[a, l, e]

            def post(k, carry, a=a, l=l, u=u):
                dst = peer(k)
                remote(
                    send_a.at[a, l, dst], recv_a.at[a, u, e], as_sem.at[a, l], ar_sem.at[a, l], (g, dst)
                ).start()
                return carry

            lax.fori_loop(1, N, post, 0)
        if l == 0:
            for cp in sib_w:
                cp.start()

    def arrived(a, l):
        blocks = recv_a.at[a, unit_of(l), pl.ds(0, N - 1)]
        return remote(blocks, blocks, as_sem.at[a, l], ar_sem.at[a, l], sib)

    acc_gu[...] = jnp.zeros_like(acc_gu)
    acc_h[...] = jnp.zeros_like(acc_h)

    def process(a, u):
        cols = pl.ds(mult(u * W, W), W)
        r = recv_a[a, u]
        late8 = r[:, 32:48, :].astype(F32)
        xa = r[:, 0:16, :].reshape(R16, U)
        xb = r[:, 16:32, :].reshape(R16, U)
        ya = late8[:, 0:8, :].reshape(R8, U).astype(BF)
        yb = late8[:, 8:16, :].reshape(R8, U).astype(BF)
        left, right = pl.ds(mult(u * W, U), U), pl.ds(mult(u * W + U, U), U)
        xm[a, :R16, left] = xa
        xm[a, R16:, left] = ya
        xm[a, :R16, right] = xb
        xm[a, R16:, right] = yb
        rows = xm[a, :, cols]
        if a == 0:
            w = jnp.concatenate([wgu[i, cols, :] for i in range(4)], axis=1)
            acc_gu[...] += mm(rows, w)
        else:
            acc_h[...] += mm(rows, wd[:, cols], 1, 1)

    def step1(a):
        blk = recv_a.at[a, z]
        return remote(blk, blk, z1s_sem.at[a], z1r_sem.at[a], at_z(first[a]))

    def step2(a, i):
        blk = recv_a.at[a, (z, first[a])[i]]
        return remote(blk, blk, z2s_sem.at[a, i], z2r_sem.at[a, i], at_z(second[a]))

    for a in range(2):
        arrived(a, 0).wait_recv()
        step1(a).start()
        step2(a, 0).start()
    for i in range(3):
        own_w[i].wait()
        sib_w[i].wait_recv()
    for a in range(2):
        process(a, z)
    for a in range(2):
        step1(a).wait_recv()
        step2(a, 1).start()
    for a in range(2):
        process(a, first[a])

    def direct(l, carry):
        for a in range(2):
            blocks = recv_a.at[a, NG + l - 1, pl.ds(0, N - 1)]
            remote(blocks, blocks, as_sem.at[a, l], ar_sem.at[a, l], sib).wait_recv()
            process(a, NG + l - 1)
        return carry

    lax.fori_loop(1, 1 + ND, direct, 0)
    for a in range(2):
        step2(a, 0).wait_recv()
        process(a, second[a])
    b_gu = remote(acc_gu, accr_gu, bs_sem.at[0], br_sem.at[0], sib)
    b_h = remote(acc_h, accr_h, bs_sem.at[1], br_sem.at[1], sib)
    step2(0, 1).wait_recv()
    process(0, zo)
    b_gu.start()
    step2(1, 1).wait_recv()
    process(1, zo)
    b_h.start()
    b_gu.wait_recv()
    b_h.wait_recv()

    RB = 64

    def act(i, carry):
        rows = pl.ds(mult(i * RB, RB), RB)
        gu = acc_gu[rows, :] + accr_gu[rows, :]
        gh = acc_h[rows, :] + accr_h[rows, :]
        gp, up = gu[:, : 2 * HID], gu[:, 2 * HID :]
        sg = jax.nn.sigmoid(gp)
        silu = gp * sg
        hid[rows, :] = (silu * up).astype(BF)
        g2[rows, : 2 * HID] = (gh * up * sg * (1.0 + gp * (1.0 - sg))).astype(BF)
        g2[rows, 2 * HID :] = (gh * silu).astype(BF)
        return carry

    lax.fori_loop(0, R // RB, act, 0)

    def row_grad(j, carry):
        cols = pl.ds(mult(j * W, W), W)
        w = jnp.concatenate([wgu[i, cols, :] for i in range(4)], axis=1)
        pack(send_c.at[j], mm(g2[...], w, 1, 1))
        recv_c[j, e] = send_c[j, e]

        def post(k, inner):
            dst = peer(k)
            remote(send_c.at[j, dst], recv_c.at[j, e], cs_sem.at[j], cr_sem.at[j], (g, dst)).start()
            return inner

        lax.fori_loop(1, N, post, 0)
        return carry

    lax.fori_loop(0, NU, row_grad, 0)

    bit1 = (((z + 1) // 2) % 2, z // 2)
    bit2 = (z // 2, z % 2)

    def rs1(j, p):
        off = mult((1 - bit1[p]) * 128, 128)
        return remote(
            zp.at[j, p, pl.ds(off, 128)], zr1.at[j, p], s1s_sem.at[j, p], s1r_sem.at[j, p], at_z(first[p])
        )

    def rs2(j, p):
        return remote(zs.at[j, p], zr2.at[j, p], s2s_sem.at[j, p], s2r_sem.at[j, p], at_z(second[p]))

    def ag1(j, p):
        blk = fin.at[j, p, pl.ds(mult(bit1[p] * 128 + bit2[p] * 64, 64), 64)]
        return remote(blk, blk, g1s_sem.at[j, p], g1r_sem.at[j, p], at_z(second[p]))

    def ag2(j, p):
        blk = fin.at[j, p, pl.ds(mult(bit1[p] * 128, 128), 128)]
        return remote(blk, blk, g2s_sem.at[j, p], g2r_sem.at[j, p], at_z(first[p]))

    def out_cols(j, p):
        return pl.ds(mult(c * H + j * W + p * U, U), U)

    def out_local(j, p):
        return pltpu.make_async_copy(fin.at[j, p], o_tok.at[:, out_cols(j, p)], ol_sem.at[j, p])

    def out_sib(j, p):
        return remote(fin.at[j, p], o_tok.at[:, out_cols(j, p)], os_sem.at[j, p], or_sem.at[j, p], sib)

    def grads_out(j):
        rows = pl.ds(mult(j * W, W), W)
        orow = pl.ds(mult(c * H + j * W, W), W)
        local, far = [], []
        for i, out in enumerate((o_gate, o_up)):
            local.append(pltpu.make_async_copy(dwgu.at[2 * i + c, rows], out.at[0, orow], dl_sem.at[j, i]))
            far.append(remote(dwgu.at[2 * i + other, rows], out.at[0, orow], ds_sem.at[j, i], dr_sem.at[j, i], sib))
        mine, yours = pl.ds(mult(c * HID, HID), HID), pl.ds(mult(other * HID, HID), HID)
        local.append(pltpu.make_async_copy(dwd.at[mine, rows], o_down.at[0, :, orow], dl_sem.at[j, 2]))
        far.append(remote(dwd.at[yours, rows], o_down.at[0, :, orow], ds_sem.at[j, 2], dr_sem.at[j, 2], sib))
        return local, far

    def pipe(t, carry):
        @pl.when(t < NU)
        def _():
            blocks = recv_c.at[t, pl.ds(0, N - 1)]
            remote(blocks, blocks, cs_sem.at[t], cr_sem.at[t], sib).wait_recv()
            r = recv_c[t]
            r8 = r[:, 32:48, :].reshape(R16, U)
            for p in range(2):
                r16 = r[:, 16 * p : 16 * p + 16, :].reshape(R16, U)
                zp[t, p] = (mm(q16[...], r16) + mm((q8a, q8b)[p][...], r8)).astype(BF)
                rs1(t, p).start()

        @pl.when((t >= 1) & (t < NU + 1))
        def _():
            j = t - 1
            for p in range(2):
                rs1(j, p).wait_recv()
                base = bit1[p] * 128
                keep = pl.ds(mult(base + bit2[p] * 64, 64), 64)
                give = pl.ds(mult(base + (1 - bit2[p]) * 64, 64), 64)
                rk = pl.ds(mult(bit2[p] * 64, 64), 64)
                rg = pl.ds(mult((1 - bit2[p]) * 64, 64), 64)
                zs[j, p] = (zp[j, p, give, :].astype(F32) + zr1[j, p, rg, :].astype(F32)).astype(BF)
                rs2(j, p).start()
                zk[j, p] = zp[j, p, keep, :].astype(F32) + zr1[j, p, rk, :].astype(F32)

        @pl.when((t >= 2) & (t < NU + 2))
        def _():
            j = t - 2
            for p in range(2):
                rs2(j, p).wait_recv()
                rows = pl.ds(mult(bit1[p] * 128 + bit2[p] * 64, 64), 64)
                fin[j, p, rows, :] = (zk[j, p] + zr2[j, p].astype(F32)).astype(BF)
                ag1(j, p).start()

        @pl.when((t >= 3) & (t < NU + 3))
        def _():
            for p in range(2):
                ag1(t - 3, p).wait_recv()
                ag2(t - 3, p).start()

        @pl.when(t >= 4)
        def _():
            for p in range(2):
                ag2(t - 4, p).wait_recv()
                out_local(t - 4, p).start()
                out_sib(t - 4, p).start()

        @pl.when(t < NU)
        def _():
            cols = pl.ds(mult(t * W, W), W)
            d1 = mm(xm[0, :, cols], g2[...], 0, 0)
            for i in range(4):
                dwgu[i, cols, :] = d1[:, i * HID : (i + 1) * HID].astype(BF)
            dwd[:, cols] = mm(hid[...], xm[1, :, cols], 0, 0).astype(BF)
            local, far = grads_out(t)
            for cp in local + far:
                cp.start()

        return carry

    lax.fori_loop(0, NU + 4, pipe, 0)

    for a in range(2):
        for l in range(1 + ND):
            arrived(a, l).wait_send()
        step1(a).wait_send()
        for i in range(2):
            step2(a, i).wait_send()
    for i in range(3):
        sib_w[i].wait_send()
    b_gu.wait_send()
    b_h.wait_send()

    def drain(j, carry):
        blocks = send_c.at[j, pl.ds(0, N - 1)]
        remote(blocks, blocks, cs_sem.at[j], cr_sem.at[j], sib).wait_send()
        for p in range(2):
            for cp in (rs1(j, p), rs2(j, p), ag1(j, p), ag2(j, p), out_sib(j, p)):
                cp.wait_send()
            out_local(j, p).wait()
            out_sib(j, p).wait_recv()
        local, far = grads_out(j)
        for cp in local:
            cp.wait()
        for cp in far:
            cp.wait()
        return carry

    lax.fori_loop(0, NU, drain, 0)


def per_device(tokens, cotangent, expert_ids, gate_scores, gate_weight, up_weight, down_weight):
    def sems(*shape):
        return pltpu.SemaphoreType.DMA(shape)

    anyspace = pl.BlockSpec(memory_space=pl.ANY)
    vmem = pl.BlockSpec(memory_space=pltpu.VMEM)
    scratch = [
        pltpu.VMEM((2, 1 + ND, T, W), BF),
        pltpu.VMEM((R, T), BF),
        pltpu.VMEM((T, R16), BF),
        pltpu.VMEM((T, R16), BF),
        pltpu.VMEM((T, R16), BF),
        pltpu.VMEM((T, 1), F32),
        pltpu.VMEM((2, 1 + ND, N, BLK, U), BF),
        pltpu.VMEM((2, NU, N, BLK, U), BF),
        pltpu.VMEM((2, R, H), BF),
        pltpu.VMEM((4, H, HID), BF),
        pltpu.VMEM((2 * HID, H), BF),
        pltpu.VMEM((R, 4 * HID), F32),
        pltpu.VMEM((R, 2 * HID), F32),
        pltpu.VMEM((R, 4 * HID), F32),
        pltpu.VMEM((R, 2 * HID), F32),
        pltpu.VMEM((R, 2 * HID), BF),
        pltpu.VMEM((R, 4 * HID), BF),
        pltpu.VMEM((NU, N, BLK, U), BF),
        pltpu.VMEM((NU, N, BLK, U), BF),
        pltpu.VMEM((NU, 2, T, U), BF),
        pltpu.VMEM((NU, 2, 128, U), BF),
        pltpu.VMEM((NU, 2, 64, U), BF),
        pltpu.VMEM((NU, 2, 64, U), F32),
        pltpu.VMEM((NU, 2, 64, U), BF),
        pltpu.VMEM((NU, 2, T, U), BF),
        pltpu.VMEM((4, H, HID), BF),
        pltpu.VMEM((2 * HID, H), BF),
        sems(2, 1 + ND), sems(3), sems(3), sems(3),
        sems(2, 1 + ND), sems(2, 1 + ND),
        sems(2), sems(2), sems(2, 2), sems(2, 2),
        sems(2), sems(2), sems(NU), sems(NU),
        sems(NU, 2), sems(NU, 2), sems(NU, 2), sems(NU, 2),
        sems(NU, 2), sems(NU, 2), sems(NU, 2), sems(NU, 2),
        sems(NU, 2), sems(NU, 2), sems(NU, 2),
        sems(NU, 3), sems(NU, 3), sems(NU, 3),
    ]
    return tuple(
        pl.pallas_call(
            body,
            out_shape=[
                jax.ShapeDtypeStruct((T, D), BF),
                jax.ShapeDtypeStruct((1, D, HID), BF),
                jax.ShapeDtypeStruct((1, D, HID), BF),
                jax.ShapeDtypeStruct((1, HID, D), BF),
            ],
            in_specs=[anyspace, anyspace, vmem, vmem, anyspace, anyspace, anyspace],
            out_specs=[anyspace] * 4,
            scratch_shapes=scratch,
            compiler_params=pltpu.CompilerParams(
                collective_id=0, has_side_effects=True, vmem_limit_bytes=60 * 1024 * 1024
            ),
            cost_estimate=pl.CostEstimate(flops=6_000_000_000, bytes_accessed=20_000_000, transcendentals=100_000),
        )(tokens, cotangent, expert_ids, gate_scores, gate_weight, up_weight, down_weight)
    )


def solution(mesh):
    placed = (
        P("ep", None),
        P("ep", None),
        P("ep", None),
        P("ep", None),
        P("ep", None, "grp"),
        P("ep", None, "grp"),
        P("ep", "grp", None),
    )
    return jax.shard_map(
        per_device,
        mesh=mesh,
        in_specs=placed,
        out_specs=(P("ep", None), P("ep", None, "grp"), P("ep", None, "grp"), P("ep", "grp", None)),
        check_vma=False,
    )
```

```python
import functools

import jax
import jax.numpy as jnp
from jax import lax
from jax.experimental import pallas as pl
from jax.experimental.pallas import tpu as pltpu
from jax.sharding import PartitionSpec as P

BF = jnp.bfloat16
F32 = jnp.float32
MESH = pl.DeviceIdType.MESH

N = 16
SIDE = 4
T = 256
HID = 128
D = 7168
H = D // 2
W = 512
U = 128
C = 2 * U
NU = H // W
NA = H // C
NP = 5
ND = NA - 2 * NP
R16 = N * 16
R8 = N * 8
R = R16 + R8
BLK = 48
OFFS = (
    (2, 2), (2, 3), (3, 2), (2, 1), (1, 2), (2, 0), (0, 2), (3, 1),
    (1, 3), (3, 3), (1, 1), (3, 0), (0, 3), (1, 0), (0, 1),
)
RB = 128
LAG = 2


def mm(a, b, ca=1, cb=0):
    return lax.dot_general(a, b, (((ca,), (cb,)), ((), ())), preferred_element_type=F32)


def pack(dst, g):
    g16 = g[:R16].reshape(N, 16, C)
    dst[:, 0:16, :] = g16[:, :, :U].astype(BF)
    dst[:, 16:32, :] = g16[:, :, U:].astype(BF)
    g8 = g[R16:].reshape(N, 8, C)
    dst[:, 32:48, :] = jnp.concatenate([g8[:, :, :U], g8[:, :, U:]], axis=1).astype(BF)


def body(
    tok, cot, ids, gs, gw, uw, dw,
    o_tok, o_gate, o_up, o_down,
    tokv, tokd, pm, q16, q8a, q8b, scale, gate_col,
    send_a, send_d, recv_a, xm, wgu, wd, acc_gu, acc_h, accr_gu, accr_h, hid, g2,
    pk, rsb, send_c, recv_c, zp, zr, fin, dwgu, dwd,
    tok_sem, tokd_sem, w_sem, ws_sem, wr_sem, as_sem, ar_sem, ds_a_sem, dr_a_sem, z1s_sem, z1r_sem, z2s_sem, z2r_sem,
    bs_sem, br_sem, ps_sem, pr_sem, cs_sem, cr_sem, xs_sem, xr_sem, gs_sem, gr_sem,
    ol_sem, os_sem, or_sem, dl_sem, ds_sem, dr_sem,
):
    g = lax.axis_index("grp")
    e = lax.axis_index("ep")
    z, c = g // 2, g % 2
    x, y = e // SIDE, e % SIDE
    other = 1 - c
    za = z + 1 - 2 * (z % 2)
    zb = 3 - z
    zo = 3 - za
    sib = (2 * z + other, e)

    def first(i):
        return za + (zb - za) * (i % 2)

    def second(i):
        return zb + (za - zb) * (i % 2)

    def at_z(zz):
        return (2 * zz + c, e)

    def peer(k):
        dx, dy = OFFS[k]
        if dx != dy:
            dx, dy = dx * other + dy * c, dy * other + dx * c
        return ((x + dx) % SIDE) * SIDE + (y + dy) % SIDE

    def remote(src, dst, ss, rs, dev):
        return pltpu.make_async_remote_copy(
            src_ref=src, dst_ref=dst, send_sem=ss, recv_sem=rs, device_id=dev, device_id_type=MESH
        )

    def mult(v, m):
        return pl.multiple_of(v, m)

    bar = pltpu.get_barrier_semaphore()
    for k in range(N - 1):
        pl.semaphore_signal(bar, inc=1, device_id=(g, peer(k)), device_id_type=MESH)
    for dev in (at_z(za), at_z(zb), sib):
        pl.semaphore_signal(bar, inc=1, device_id=dev, device_id_type=MESH)

    def load(src):
        col = mult(c * H + (z % 2) * NP * C, C)
        return pltpu.make_async_copy(src.at[:, pl.ds(col, NP * C)], tokv, tok_sem)

    def load_d(a):
        col = mult(c * H + 2 * NP * C, C)
        return pltpu.make_async_copy((tok, cot)[a].at[:, pl.ds(col, ND * C)], tokd.at[a], tokd_sem.at[a])

    @pl.when(z < 2)
    def _():
        load(tok).start()

    @pl.when(z >= 2)
    def _():
        load(cot).start()

    for a in range(2):
        load_d(a).start()

    my_half = mult(c * H, H)
    own_w = [
        pltpu.make_async_copy(gw.at[0, pl.ds(my_half, H)], wgu.at[c], w_sem.at[0]),
        pltpu.make_async_copy(uw.at[0, pl.ds(my_half, H)], wgu.at[2 + c], w_sem.at[1]),
        pltpu.make_async_copy(
            dw.at[0, :, pl.ds(my_half, H)], wd.at[pl.ds(mult(c * HID, HID), HID)], w_sem.at[2]
        ),
    ]
    for cp in own_w:
        cp.start()

    def column(row):
        return jnp.transpose(jnp.broadcast_to(row, (128, T)))[:, 0:1]

    idf = ids[...].astype(F32)
    e_row = jnp.min(idf, axis=0, keepdims=True)
    e_col = column(e_row)
    sub = lax.broadcasted_iota(jnp.int32, (T, T), 0)
    lane = lax.broadcasted_iota(jnp.int32, (T, T), 1)
    before = jnp.where(sub < lane, jnp.where(e_col == e_row, 1.0, 0.0), 0.0)
    rank_row = jnp.sum(before, axis=0, keepdims=True)
    valid = e_row < N
    slot16 = jnp.where(valid & (rank_row < 16), e_row * 16 + rank_row, -1.0)
    slot8 = jnp.where(valid & (rank_row >= 16), e_row * 8 + (rank_row - 16), -1.0)

    def onehot(test):
        return jnp.where(test, 1.0, 0.0).astype(BF)

    subf = sub.astype(F32)
    pm[:R16, :] = onehot(subf == slot16)
    pm[R16:, :] = onehot(subf[:R8] == slot8)
    gate_row = jnp.sum(jnp.where(idf < N, gs[...], 0.0), axis=0, keepdims=True)
    gate_col[...] = column(gate_row)
    scale[...] = column(jnp.where(z < 2, jnp.ones_like(gate_row), gate_row))

    pl.semaphore_wait(bar, N - 1 + 3)

    their_half = mult(other * H, H)
    sib_w = [
        remote(gw.at[0, pl.ds(their_half, H)], wgu.at[c], ws_sem.at[0], wr_sem.at[0], sib),
        remote(uw.at[0, pl.ds(their_half, H)], wgu.at[2 + c], ws_sem.at[1], wr_sem.at[1], sib),
        remote(
            dw.at[0, :, pl.ds(their_half, H)],
            wd.at[pl.ds(mult(c * HID, HID), HID)],
            ws_sem.at[2], wr_sem.at[2], sib,
        ),
    ]

    for cp in sib_w:
        cp.start()

    def spread(buf, n, ss, rs):
        recv_a[n, e] = buf[e]
        for k in range(N - 1):
            dst = peer(k)
            remote(buf.at[dst], recv_a.at[n, e], ss, rs, (g, dst)).start()

    def part_of(owner, i):
        return (owner // 2) * NA + (owner % 2) * NP + i

    def dispatch(i, carry):
        src = tokv[:, pl.ds(mult(i * C, C), C)]
        src = (scale[...] * src.astype(F32)).astype(BF)
        pack(send_a.at[i], mm(pm[...], src))
        spread(send_a.at[i], part_of(z, i), as_sem.at[i], ar_sem.at[i])
        return carry

    def dispatch_d(d):
        for a in range(2):
            src = tokd[a, :, pl.ds(mult(d * C, C), C)]
            if a == 1:
                src = (gate_col[...] * src.astype(F32)).astype(BF)
            pack(send_d.at[a, d], mm(pm[...], src))
            spread(send_d.at[a, d], a * NA + 2 * NP + d, ds_a_sem.at[a, d], dr_a_sem.at[a, d])

    load(tok).wait()
    lax.fori_loop(0, NP, dispatch, 0)
    for a in range(2):
        load_d(a).wait()

    lanef = lane.astype(F32)
    q16[...] = onehot(lanef == column(slot16))
    late_a = jnp.where(valid & (rank_row >= 16), e_row * 16 + (rank_row - 16), -16.0)
    q8a[...] = onehot(lanef == column(late_a))
    q8b[...] = onehot(lanef == column(late_a + 8))
    acc_gu[...] = jnp.zeros_like(acc_gu)
    acc_h[...] = jnp.zeros_like(acc_h)

    def arrived(i):
        blocks = recv_a.at[part_of(z, i), pl.ds(0, N - 1)]
        return remote(blocks, blocks, as_sem.at[i], ar_sem.at[i], sib)

    def arrived_d(a, d):
        blocks = recv_a.at[a * NA + 2 * NP + d, pl.ds(0, N - 1)]
        return remote(blocks, blocks, ds_a_sem.at[a, d], dr_a_sem.at[a, d], sib)

    def unpack(a, m):
        r = recv_a[a * NA + m]
        late8 = r[:, 32:48, :].astype(F32)
        left, right = pl.ds(mult(m * C, U), U), pl.ds(mult(m * C + U, U), U)
        xm[a, :R16, left] = r[:, 0:16, :].reshape(R16, U)
        xm[a, R16:, left] = late8[:, 0:8, :].reshape(R8, U).astype(BF)
        xm[a, :R16, right] = r[:, 16:32, :].reshape(R16, U)
        xm[a, R16:, right] = late8[:, 8:16, :].reshape(R8, U).astype(BF)

    def multiply(a, m):
        cols = pl.ds(mult(m * C, C), C)
        if a == 0:
            w = jnp.concatenate([wgu[k, cols, :] for k in range(4)], axis=1)
            acc_gu[...] += mm(xm[0, :, cols], w)
        else:
            acc_h[...] += mm(xm[1, :, cols], wd[:, cols], 1, 1)

    def process_of(owner, i):
        a, m = owner // 2, (owner % 2) * NP + i
        unpack(a, m)

        @pl.when(a == 0)
        def _():
            multiply(0, m)

        @pl.when(a == 1)
        def _():
            multiply(1, m)

    def process_d(d):
        for a in range(2):
            arrived_d(a, d).wait_recv()
            unpack(a, 2 * NP + d)
            multiply(a, 2 * NP + d)

    def step1(i):
        blk = recv_a.at[part_of(z, i)]
        return remote(blk, blk, z1s_sem.at[i], z1r_sem.at[i], at_z(first(i)))

    def step2(i, fwd):
        blk = recv_a.at[part_of(first(i), i) if fwd else part_of(z, i)]
        return remote(blk, blk, z2s_sem.at[i, fwd], z2r_sem.at[i, fwd], at_z(second(i)))

    dispatch_d(0)

    def gather1(i, carry):
        arrived(i).wait_recv()
        step1(i).start()
        step2(i, 0).start()

        @pl.when(i + 1 < ND)
        def _():
            dispatch_d(i + 1)

        return carry

    lax.fori_loop(0, NP, gather1, 0)
    for d in range(NP + 1, ND):
        dispatch_d(d)
    for k in range(3):
        own_w[k].wait()
        sib_w[k].wait_recv()

    def gather2(i, carry):
        step1(i).wait_recv()
        step2(i, 1).start()
        process_of(z, i)
        process_of(first(i), i)

        @pl.when(i < ND)
        def _():
            process_d(i)

        return carry

    lax.fori_loop(0, NP, gather2, 0)

    def gather3(i, carry):
        @pl.when(i + NP < ND)
        def _():
            process_d(i + NP)

        step2(i, 0).wait_recv()
        process_of(second(i), i)
        step2(i, 1).wait_recv()
        process_of(zo, i)
        return carry

    lax.fori_loop(0, NP, gather3, 0)

    def swap(i):
        rows = pl.ds(mult(i * RB, RB), RB)
        return (
            remote(acc_gu.at[rows], accr_gu.at[rows], bs_sem.at[0, i], br_sem.at[0, i], sib),
            remote(acc_h.at[rows], accr_h.at[rows], bs_sem.at[1, i], br_sem.at[1, i], sib),
        )

    for i in range(R // RB):
        for cp in swap(i):
            cp.start()

    def act(i, carry):
        rows = pl.ds(mult(i * RB, RB), RB)
        for cp in swap(i):
            cp.wait_recv()
        gu = acc_gu[rows, :] + accr_gu[rows, :]
        gh = acc_h[rows, :] + accr_h[rows, :]
        gp, up = gu[:, : 2 * HID], gu[:, 2 * HID :]
        sg = jax.nn.sigmoid(gp)
        silu = gp * sg
        hid[rows, :] = (silu * up).astype(BF)
        g2[rows, : 2 * HID] = (gh * up * sg * (1.0 + gp * (1.0 - sg))).astype(BF)
        g2[rows, 2 * HID :] = (gh * silu).astype(BF)
        return carry

    lax.fori_loop(0, R // RB, act, 0)

    def half(j):
        b = ((z + 1) // 2) % 2
        return b + (z // 2 - b) * (j % 2)

    def pair(j):
        return remote(pk.at[j, 1 - half(j)], rsb.at[j], ps_sem.at[j], pr_sem.at[j], at_z(first(j)))

    def row_grad(j, carry):
        cols = pl.ds(mult(j * W, W), W)
        w = jnp.concatenate([wgu[i, cols, :] for i in range(4)], axis=1)
        r = mm(g2[...], w, 1, 1)
        for h in range(2):
            pack(pk.at[j, h], r[:, h * C : (h + 1) * C])
        pair(j).start()
        return carry

    lax.fori_loop(0, NU, row_grad, 0)

    def back(j, carry):
        pair(j).wait_recv()
        send_c[j] = (pk[j, half(j)].astype(F32) + rsb[j].astype(F32)).astype(BF)
        recv_c[j, e] = send_c[j, e]
        for k in range(N - 1):
            dst = peer(k)
            remote(send_c.at[j, dst], recv_c.at[j, e], cs_sem.at[j], cr_sem.at[j], (g, dst)).start()
        return carry

    lax.fori_loop(0, NU, back, 0)

    def cross(j):
        return remote(zp.at[j], zr.at[j], xs_sem.at[j], xr_sem.at[j], at_z(second(j)))

    def whole(j):
        blk = fin.at[j, half(j)]
        return remote(blk, blk, gs_sem.at[j], gr_sem.at[j], at_z(first(j)))

    def out_cols(j, p):
        return pl.ds(mult(c * H + j * W + p * C, C), C)

    def out_local(j, p):
        return pltpu.make_async_copy(fin.at[j, p], o_tok.at[:, out_cols(j, p)], ol_sem.at[j, p])

    def out_sib(j, p):
        return remote(fin.at[j, p], o_tok.at[:, out_cols(j, p)], os_sem.at[j, p], or_sem.at[j, p], sib)

    def grads_out(j):
        rows = pl.ds(mult(j * W, W), W)
        orow = pl.ds(mult(c * H + j * W, W), W)
        local, far = [], []
        for i, out in enumerate((o_gate, o_up)):
            local.append(pltpu.make_async_copy(dwgu.at[2 * i + c, rows], out.at[0, orow], dl_sem.at[j, i]))
            far.append(remote(dwgu.at[2 * i + other, rows], out.at[0, orow], ds_sem.at[j, i], dr_sem.at[j, i], sib))
        mine, yours = pl.ds(mult(c * HID, HID), HID), pl.ds(mult(other * HID, HID), HID)
        local.append(pltpu.make_async_copy(dwd.at[mine, rows], o_down.at[0, :, orow], dl_sem.at[j, 2]))
        far.append(remote(dwd.at[yours, rows], o_down.at[0, :, orow], ds_sem.at[j, 2], dr_sem.at[j, 2], sib))
        return local, far

    def pipe(t, carry):
        @pl.when(t < NU)
        def _():
            blocks = recv_c.at[t, pl.ds(0, N - 1)]
            remote(blocks, blocks, cs_sem.at[t], cr_sem.at[t], sib).wait_recv()
            r = recv_c[t]
            r8 = r[:, 32:48, :].reshape(R16, U)
            for p in range(2):
                r16 = r[:, 16 * p : 16 * p + 16, :].reshape(R16, U)
                zp[t, :, p * U : (p + 1) * U] = (mm(q16[...], r16) + mm((q8a, q8b)[p][...], r8)).astype(BF)
            cross(t).start()

        @pl.when((t >= LAG) & (t < NU + LAG))
        def _():
            j = t - LAG
            cross(j).wait_recv()
            fin[j, half(j)] = (zp[j].astype(F32) + zr[j].astype(F32)).astype(BF)
            whole(j).start()

        @pl.when(t >= 2 * LAG)
        def _():
            whole(t - 2 * LAG).wait_recv()
            for p in range(2):
                out_local(t - 2 * LAG, p).start()
                out_sib(t - 2 * LAG, p).start()

        @pl.when(t < NU)
        def _():
            cols = pl.ds(mult(t * W, W), W)
            d1 = mm(xm[0, :, cols], g2[...], 0, 0)
            for i in range(4):
                dwgu[i, cols, :] = d1[:, i * HID : (i + 1) * HID].astype(BF)
            dwd[:, cols] = mm(hid[...], xm[1, :, cols], 0, 0).astype(BF)
            local, far = grads_out(t)
            for cp in local + far:
                cp.start()

        return carry

    lax.fori_loop(0, NU + 2 * LAG, pipe, 0)

    for i in range(3):
        sib_w[i].wait_send()
        for cp in swap(i):
            cp.wait_send()

    def drain_a(i, carry):
        arrived(i).wait_send()
        step1(i).wait_send()
        step2(i, 0).wait_send()
        step2(i, 1).wait_send()
        return carry

    lax.fori_loop(0, NP, drain_a, 0)
    for d in range(ND):
        for a in range(2):
            arrived_d(a, d).wait_send()

    def drain(j, carry):
        blocks = send_c.at[j, pl.ds(0, N - 1)]
        remote(blocks, blocks, cs_sem.at[j], cr_sem.at[j], sib).wait_send()
        for cp in (pair(j), cross(j), whole(j)):
            cp.wait_send()
        for p in range(2):
            out_local(j, p).wait()
            out_sib(j, p).wait()
        local, far = grads_out(j)
        for cp in local + far:
            cp.wait()
        return carry

    lax.fori_loop(0, NU, drain, 0)


def write_out(*refs):
    sem = refs[8]
    copies = [pltpu.make_async_copy(refs[i], refs[4 + i], sem.at[i]) for i in range(4)]
    for cp in copies:
        cp.start()
    for cp in copies:
        cp.wait()


def per_device(tokens, cotangent, expert_ids, gate_scores, gate_weight, up_weight, down_weight):
    def sems(*shape):
        return pltpu.SemaphoreType.DMA(shape)

    anyspace = pl.BlockSpec(memory_space=pl.ANY)
    vmem = pl.BlockSpec(memory_space=pltpu.VMEM)
    scratch = [
        pltpu.VMEM((T, NP * C), BF),
        pltpu.VMEM((2, T, ND * C), BF),
        pltpu.VMEM((R, T), BF),
        pltpu.VMEM((T, R16), BF),
        pltpu.VMEM((T, R16), BF),
        pltpu.VMEM((T, R16), BF),
        pltpu.VMEM((T, 1), F32),
        pltpu.VMEM((T, 1), F32),
        pltpu.VMEM((NP, N, BLK, U), BF),
        pltpu.VMEM((2, ND, N, BLK, U), BF),
        pltpu.VMEM((2 * NA, N, BLK, U), BF),
        pltpu.VMEM((2, R, H), BF),
        pltpu.VMEM((4, H, HID), BF),
        pltpu.VMEM((2 * HID, H), BF),
        pltpu.VMEM((R, 4 * HID), F32),
        pltpu.VMEM((R, 2 * HID), F32),
        pltpu.VMEM((R, 4 * HID), F32),
        pltpu.VMEM((R, 2 * HID), F32),
        pltpu.VMEM((R, 2 * HID), BF),
        pltpu.VMEM((R, 4 * HID), BF),
        pltpu.VMEM((NU, 2, N, BLK, U), BF),
        pltpu.VMEM((NU, N, BLK, U), BF),
        pltpu.VMEM((NU, N, BLK, U), BF),
        pltpu.VMEM((NU, N, BLK, U), BF),
        pltpu.VMEM((NU, T, C), BF),
        pltpu.VMEM((NU, T, C), BF),
        pltpu.VMEM((NU, 2, T, C), BF),
        pltpu.VMEM((4, H, HID), BF),
        pltpu.VMEM((2 * HID, H), BF),
        pltpu.SemaphoreType.DMA, sems(2), sems(3), sems(3), sems(3),
        sems(NP), sems(NP), sems(2, ND), sems(2, ND), sems(NP), sems(NP), sems(NP, 2), sems(NP, 2),
        sems(2, R // RB), sems(2, R // RB),
        sems(NU), sems(NU), sems(NU), sems(NU), sems(NU), sems(NU), sems(NU), sems(NU),
        sems(NU, 2), sems(NU, 2), sems(NU, 2),
        sems(NU, 3), sems(NU, 3), sems(NU, 3),
    ]
    shapes = [((T, D), BF), ((1, D, HID), BF), ((1, D, HID), BF), ((1, HID, D), BF)]
    held = pl.pallas_call(
        body,
        out_shape=[pltpu.VMEM(*shape) for shape in shapes],
        in_specs=[anyspace, anyspace, vmem, vmem, anyspace, anyspace, anyspace],
        out_specs=[anyspace] * 4,
        scratch_shapes=scratch,
        compiler_params=pltpu.CompilerParams(
            collective_id=0, has_side_effects=True, vmem_limit_bytes=47 * 1024 * 1024
        ),
        cost_estimate=pl.CostEstimate(flops=6_000_000_000, bytes_accessed=20_000_000, transcendentals=100_000),
    )(tokens, cotangent, expert_ids.T, gate_scores.T, gate_weight, up_weight, down_weight)
    held = [pltpu.with_memory_space_constraint(h, pltpu.VMEM) for h in held]
    return tuple(
        pl.pallas_call(
            write_out,
            out_shape=[jax.ShapeDtypeStruct(*shape) for shape in shapes],
            in_specs=[anyspace] * 4,
            out_specs=[anyspace] * 4,
            scratch_shapes=[sems(4)],
            compiler_params=pltpu.CompilerParams(vmem_limit_bytes=2 * 1024 * 1024),
        )(*held)
    )


def solution(mesh):
    placed = (
        P("ep", None),
        P("ep", None),
        P("ep", None),
        P("ep", None),
        P("ep", None, "grp"),
        P("ep", None, "grp"),
        P("ep", "grp", None),
    )
    return jax.shard_map(
        per_device,
        mesh=mesh,
        in_specs=placed,
        out_specs=(P("ep", None), P("ep", None, "grp"), P("ep", None, "grp"), P("ep", "grp", None)),
        check_vma=False,
    )
```

```python
import functools

import jax
import jax.numpy as jnp
from jax import lax
from jax.experimental import pallas as pl
from jax.experimental.pallas import tpu as pltpu
from jax.sharding import PartitionSpec as P

BF = jnp.bfloat16
F32 = jnp.float32
MESH = pl.DeviceIdType.MESH

N = 16
SIDE = 4
T = 256
HID = 128
D = 7168
H = D // 2
W = 512
U = 128
C = 2 * U
NU = H // W
NA = H // C
NP = 5
ND = 6
R16 = N * 16
R8 = N * 8
R = R16 + R8
BLK = 48
OFFS = (
    (2, 2), (2, 3), (3, 2), (2, 1), (1, 2), (2, 0), (0, 2), (3, 1),
    (1, 3), (3, 3), (1, 1), (3, 0), (0, 3), (1, 0), (0, 1),
)
RB = 128
LAG = 2


def mm(a, b, ca=1, cb=0):
    return lax.dot_general(a, b, (((ca,), (cb,)), ((), ())), preferred_element_type=F32)


def pack(dst, g):
    g16 = g[:R16].reshape(N, 16, C)
    dst[:, 0:16, :] = g16[:, :, :U].astype(BF)
    dst[:, 16:32, :] = g16[:, :, U:].astype(BF)
    g8 = g[R16:].reshape(N, 8, C)
    dst[:, 32:48, :] = jnp.concatenate([g8[:, :, :U], g8[:, :, U:]], axis=1).astype(BF)


def body(
    tok, cot, ids, gs, gw, uw, dw,
    o_tok, o_gate, o_up, o_down,
    tokv, tokd, pm, q16, q8a, q8b, scale, gate_col,
    send_a, send_d, recv_a, xm, wgu, wd, acc_gu, acc_h, accr_gu, accr_h, hid, g2,
    pk, rsb, send_c, recv_c, zp, zr, fin, dwgu, dwd,
    tok_sem, tokd_sem, w_sem, ws_sem, wr_sem, as_sem, ar_sem, ds_a_sem, dr_a_sem, z1s_sem, z1r_sem, z2s_sem, z2r_sem,
    bs_sem, br_sem, ps_sem, pr_sem, cs_sem, cr_sem, xs_sem, xr_sem, gs_sem, gr_sem,
    ol_sem, os_sem, or_sem, dl_sem, ds_sem, dr_sem,
):
    g = lax.axis_index("grp")
    e = lax.axis_index("ep")
    z, c = g // 2, g % 2
    x, y = e // SIDE, e % SIDE
    other = 1 - c
    npc = NP - c
    ndc = NA - 2 * npc
    za = z + 1 - 2 * (z % 2)
    zb = 3 - z
    zo = 3 - za
    sib = (2 * z + other, e)

    def first(i):
        return za + (zb - za) * ((i + c) % 2)

    def second(i):
        return zb + (za - zb) * ((i + c) % 2)

    def at_z(zz):
        return (2 * zz + c, e)

    def peer(k):
        dx, dy = OFFS[k]
        if dx != dy:
            dx, dy = dx * other + dy * c, dy * other + dx * c
        return ((x + dx) % SIDE) * SIDE + (y + dy) % SIDE

    def remote(src, dst, ss, rs, dev):
        return pltpu.make_async_remote_copy(
            src_ref=src, dst_ref=dst, send_sem=ss, recv_sem=rs, device_id=dev, device_id_type=MESH
        )

    def mult(v, m):
        return pl.multiple_of(v, m)

    bar = pltpu.get_barrier_semaphore()
    for k in range(N - 1):
        pl.semaphore_signal(bar, inc=1, device_id=(g, peer(k)), device_id_type=MESH)
    for dev in (at_z(za), at_z(zb), sib):
        pl.semaphore_signal(bar, inc=1, device_id=dev, device_id_type=MESH)

    def load(src):
        col = mult(c * H + (z % 2) * npc * C, C)
        return pltpu.make_async_copy(src.at[:, pl.ds(col, NP * C)], tokv, tok_sem)

    def load_d(a):
        col = mult(c * H + 2 * npc * C, C)
        return pltpu.make_async_copy((tok, cot)[a].at[:, pl.ds(col, ND * C)], tokd.at[a], tokd_sem.at[a])

    @pl.when(z < 2)
    def _():
        load(tok).start()

    @pl.when(z >= 2)
    def _():
        load(cot).start()

    for a in range(2):
        load_d(a).start()

    my_half = mult(c * H, H)
    own_w = [
        pltpu.make_async_copy(gw.at[0, pl.ds(my_half, H)], wgu.at[c], w_sem.at[0]),
        pltpu.make_async_copy(uw.at[0, pl.ds(my_half, H)], wgu.at[2 + c], w_sem.at[1]),
        pltpu.make_async_copy(
            dw.at[0, :, pl.ds(my_half, H)], wd.at[pl.ds(mult(c * HID, HID), HID)], w_sem.at[2]
        ),
    ]
    for cp in own_w:
        cp.start()

    def column(row):
        return jnp.transpose(jnp.broadcast_to(row, (128, T)))[:, 0:1]

    idf = ids[...].astype(F32)
    e_row = jnp.min(idf, axis=0, keepdims=True)
    e_col = column(e_row)
    sub = lax.broadcasted_iota(jnp.int32, (T, T), 0)
    lane = lax.broadcasted_iota(jnp.int32, (T, T), 1)
    before = jnp.where(sub < lane, jnp.where(e_col == e_row, 1.0, 0.0), 0.0)
    rank_row = jnp.sum(before, axis=0, keepdims=True)
    valid = e_row < N
    slot16 = jnp.where(valid & (rank_row < 16), e_row * 16 + rank_row, -1.0)
    slot8 = jnp.where(valid & (rank_row >= 16), e_row * 8 + (rank_row - 16), -1.0)

    def onehot(test):
        return jnp.where(test, 1.0, 0.0).astype(BF)

    subf = sub.astype(F32)
    pm[:R16, :] = onehot(subf == slot16)
    pm[R16:, :] = onehot(subf[:R8] == slot8)
    gate_row = jnp.sum(jnp.where(idf < N, gs[...], 0.0), axis=0, keepdims=True)
    gate_col[...] = column(gate_row)
    scale[...] = column(jnp.where(z < 2, jnp.ones_like(gate_row), gate_row))

    pl.semaphore_wait(bar, N - 1 + 3)

    their_half = mult(other * H, H)
    sib_w = [
        remote(gw.at[0, pl.ds(their_half, H)], wgu.at[c], ws_sem.at[0], wr_sem.at[0], sib),
        remote(uw.at[0, pl.ds(their_half, H)], wgu.at[2 + c], ws_sem.at[1], wr_sem.at[1], sib),
        remote(
            dw.at[0, :, pl.ds(their_half, H)],
            wd.at[pl.ds(mult(c * HID, HID), HID)],
            ws_sem.at[2], wr_sem.at[2], sib,
        ),
    ]

    for cp in sib_w:
        cp.start()

    def spread(buf, n, ss, rs):
        recv_a[n, e] = buf[e]
        for k in range(N - 1):
            dst = peer(k)
            remote(buf.at[dst], recv_a.at[n, e], ss, rs, (g, dst)).start()

    def part_of(owner, i):
        return (owner // 2) * NA + (owner % 2) * npc + i

    def dispatch(i, carry):
        src = tokv[:, pl.ds(mult(i * C, C), C)]
        src = (scale[...] * src.astype(F32)).astype(BF)
        pack(send_a.at[i], mm(pm[...], src))
        spread(send_a.at[i], part_of(z, i), as_sem.at[i], ar_sem.at[i])
        return carry

    def dispatch_d(d, carry=0):
        for a in range(2):
            src = tokd[a, :, pl.ds(mult(d * C, C), C)]
            if a == 1:
                src = (gate_col[...] * src.astype(F32)).astype(BF)
            pack(send_d.at[a, d], mm(pm[...], src))
            spread(send_d.at[a, d], a * NA + 2 * npc + d, ds_a_sem.at[a, d], dr_a_sem.at[a, d])
        return carry

    load(tok).wait()
    lax.fori_loop(0, npc, dispatch, 0)
    for a in range(2):
        load_d(a).wait()

    lanef = lane.astype(F32)
    q16[...] = onehot(lanef == column(slot16))
    late_a = jnp.where(valid & (rank_row >= 16), e_row * 16 + (rank_row - 16), -16.0)
    q8a[...] = onehot(lanef == column(late_a))
    q8b[...] = onehot(lanef == column(late_a + 8))
    acc_gu[...] = jnp.zeros_like(acc_gu)
    acc_h[...] = jnp.zeros_like(acc_h)

    def arrived(i):
        blocks = recv_a.at[part_of(z, i), pl.ds(0, N - 1)]
        return remote(blocks, blocks, as_sem.at[i], ar_sem.at[i], sib)

    def arrived_d(a, d):
        blocks = recv_a.at[a * NA + 2 * npc + d, pl.ds(0, N - 1)]
        return remote(blocks, blocks, ds_a_sem.at[a, d], dr_a_sem.at[a, d], sib)

    def unpack(a, m):
        r = recv_a[a * NA + m]
        late8 = r[:, 32:48, :].astype(F32)
        left, right = pl.ds(mult(m * C, U), U), pl.ds(mult(m * C + U, U), U)
        xm[a, :R16, left] = r[:, 0:16, :].reshape(R16, U)
        xm[a, R16:, left] = late8[:, 0:8, :].reshape(R8, U).astype(BF)
        xm[a, :R16, right] = r[:, 16:32, :].reshape(R16, U)
        xm[a, R16:, right] = late8[:, 8:16, :].reshape(R8, U).astype(BF)

    def multiply(a, m):
        cols = pl.ds(mult(m * C, C), C)
        if a == 0:
            w = jnp.concatenate([wgu[k, cols, :] for k in range(4)], axis=1)
            acc_gu[...] += mm(xm[0, :, cols], w)
        else:
            acc_h[...] += mm(xm[1, :, cols], wd[:, cols], 1, 1)

    def process_of(owner, i):
        a, m = owner // 2, (owner % 2) * npc + i
        unpack(a, m)

        @pl.when(a == 0)
        def _():
            multiply(0, m)

        @pl.when(a == 1)
        def _():
            multiply(1, m)

    def process_d(d):
        for a in range(2):
            arrived_d(a, d).wait_recv()
            unpack(a, 2 * npc + d)
            multiply(a, 2 * npc + d)

    def step1(i):
        blk = recv_a.at[part_of(z, i)]
        return remote(blk, blk, z1s_sem.at[i], z1r_sem.at[i], at_z(first(i)))

    def step2(i, fwd):
        blk = recv_a.at[part_of(first(i), i) if fwd else part_of(z, i)]
        return remote(blk, blk, z2s_sem.at[i, fwd], z2r_sem.at[i, fwd], at_z(second(i)))

    dispatch_d(0)

    def gather1(i, carry):
        arrived(i).wait_recv()
        step1(i).start()
        step2(i, 0).start()

        @pl.when(i + 1 < ndc)
        def _():
            dispatch_d(i + 1)

        return carry

    lax.fori_loop(0, npc, gather1, 0)
    lax.fori_loop(npc + 1, ndc, dispatch_d, 0)
    for k in range(3):
        own_w[k].wait()
        sib_w[k].wait_recv()

    def gather2(i, carry):
        step1(i).wait_recv()
        step2(i, 1).start()
        process_of(z, i)
        process_of(first(i), i)

        @pl.when(i < ndc)
        def _():
            process_d(i)

        return carry

    lax.fori_loop(0, npc, gather2, 0)

    def gather3(i, carry):
        @pl.when(i + npc < ndc)
        def _():
            process_d(i + npc)

        step2(i, 0).wait_recv()
        process_of(second(i), i)
        step2(i, 1).wait_recv()
        process_of(zo, i)
        return carry

    lax.fori_loop(0, npc, gather3, 0)

    def swap(i):
        rows = pl.ds(mult(i * RB, RB), RB)
        return (
            remote(acc_gu.at[rows], accr_gu.at[rows], bs_sem.at[0, i], br_sem.at[0, i], sib),
            remote(acc_h.at[rows], accr_h.at[rows], bs_sem.at[1, i], br_sem.at[1, i], sib),
        )

    for i in range(R // RB):
        for cp in swap(i):
            cp.start()

    def act(i, carry):
        rows = pl.ds(mult(i * RB, RB), RB)
        for cp in swap(i):
            cp.wait_recv()
        gu = acc_gu[rows, :] + accr_gu[rows, :]
        gh = acc_h[rows, :] + accr_h[rows, :]
        gp, up = gu[:, : 2 * HID], gu[:, 2 * HID :]
        sg = jax.nn.sigmoid(gp)
        silu = gp * sg
        hid[rows, :] = (silu * up).astype(BF)
        g2[rows, : 2 * HID] = (gh * up * sg * (1.0 + gp * (1.0 - sg))).astype(BF)
        g2[rows, 2 * HID :] = (gh * silu).astype(BF)
        return carry

    lax.fori_loop(0, R // RB, act, 0)

    def half(j):
        b = ((z + 1) // 2) % 2
        return b + (z // 2 - b) * ((j + c) % 2)

    def pair(j):
        return remote(pk.at[j, 1 - half(j)], rsb.at[j], ps_sem.at[j], pr_sem.at[j], at_z(first(j)))

    def row_grad(j, carry):
        cols = pl.ds(mult(j * W, W), W)
        w = jnp.concatenate([wgu[i, cols, :] for i in range(4)], axis=1)
        r = mm(g2[...], w, 1, 1)
        for h in range(2):
            pack(pk.at[j, h], r[:, h * C : (h + 1) * C])
        pair(j).start()
        return carry

    lax.fori_loop(0, NU, row_grad, 0)

    def back(j, carry):
        pair(j).wait_recv()
        send_c[j] = (pk[j, half(j)].astype(F32) + rsb[j].astype(F32)).astype(BF)
        recv_c[j, e] = send_c[j, e]
        for k in range(N - 1):
            dst = peer(k)
            remote(send_c.at[j, dst], recv_c.at[j, e], cs_sem.at[j], cr_sem.at[j], (g, dst)).start()
        return carry

    lax.fori_loop(0, NU, back, 0)

    def cross(j):
        return remote(zp.at[j], zr.at[j], xs_sem.at[j], xr_sem.at[j], at_z(second(j)))

    def whole(j):
        blk = fin.at[j, half(j)]
        return remote(blk, blk, gs_sem.at[j], gr_sem.at[j], at_z(first(j)))

    def out_cols(j, p):
        return pl.ds(mult(c * H + j * W + p * C, C), C)

    def out_local(j, p):
        return pltpu.make_async_copy(fin.at[j, p], o_tok.at[:, out_cols(j, p)], ol_sem.at[j, p])

    def out_sib(j, p):
        return remote(fin.at[j, p], o_tok.at[:, out_cols(j, p)], os_sem.at[j, p], or_sem.at[j, p], sib)

    def grads_out(j):
        rows = pl.ds(mult(j * W, W), W)
        orow = pl.ds(mult(c * H + j * W, W), W)
        local, far = [], []
        for i, out in enumerate((o_gate, o_up)):
            local.append(pltpu.make_async_copy(dwgu.at[2 * i + c, rows], out.at[0, orow], dl_sem.at[j, i]))
            far.append(remote(dwgu.at[2 * i + other, rows], out.at[0, orow], ds_sem.at[j, i], dr_sem.at[j, i], sib))
        mine, yours = pl.ds(mult(c * HID, HID), HID), pl.ds(mult(other * HID, HID), HID)
        local.append(pltpu.make_async_copy(dwd.at[mine, rows], o_down.at[0, :, orow], dl_sem.at[j, 2]))
        far.append(remote(dwd.at[yours, rows], o_down.at[0, :, orow], ds_sem.at[j, 2], dr_sem.at[j, 2], sib))
        return local, far

    def pipe(t, carry):
        @pl.when(t < NU)
        def _():
            blocks = recv_c.at[t, pl.ds(0, N - 1)]
            remote(blocks, blocks, cs_sem.at[t], cr_sem.at[t], sib).wait_recv()
            r = recv_c[t]
            r8 = r[:, 32:48, :].reshape(R16, U)
            for p in range(2):
                r16 = r[:, 16 * p : 16 * p + 16, :].reshape(R16, U)
                zp[t, :, p * U : (p + 1) * U] = (mm(q16[...], r16) + mm((q8a, q8b)[p][...], r8)).astype(BF)
            cross(t).start()

        @pl.when((t >= LAG) & (t < NU + LAG))
        def _():
            j = t - LAG
            cross(j).wait_recv()
            fin[j, half(j)] = (zp[j].astype(F32) + zr[j].astype(F32)).astype(BF)
            whole(j).start()

        @pl.when(t >= 2 * LAG)
        def _():
            whole(t - 2 * LAG).wait_recv()
            for p in range(2):
                out_local(t - 2 * LAG, p).start()
                out_sib(t - 2 * LAG, p).start()

        @pl.when(t < NU)
        def _():
            cols = pl.ds(mult(t * W, W), W)
            d1 = mm(xm[0, :, cols], g2[...], 0, 0)
            for i in range(4):
                dwgu[i, cols, :] = d1[:, i * HID : (i + 1) * HID].astype(BF)
            dwd[:, cols] = mm(hid[...], xm[1, :, cols], 0, 0).astype(BF)
            local, far = grads_out(t)
            for cp in local + far:
                cp.start()

        return carry

    lax.fori_loop(0, NU + 2 * LAG, pipe, 0)

    for i in range(3):
        sib_w[i].wait_send()
        for cp in swap(i):
            cp.wait_send()

    def drain_a(i, carry):
        arrived(i).wait_send()
        step1(i).wait_send()
        step2(i, 0).wait_send()
        step2(i, 1).wait_send()
        return carry

    lax.fori_loop(0, npc, drain_a, 0)

    def drain_d(d, carry):
        for a in range(2):
            arrived_d(a, d).wait_send()
        return carry

    lax.fori_loop(0, ndc, drain_d, 0)

    def drain(j, carry):
        blocks = send_c.at[j, pl.ds(0, N - 1)]
        remote(blocks, blocks, cs_sem.at[j], cr_sem.at[j], sib).wait_send()
        for cp in (pair(j), cross(j), whole(j)):
            cp.wait_send()
        for p in range(2):
            out_local(j, p).wait()
            out_sib(j, p).wait()
        local, far = grads_out(j)
        for cp in local + far:
            cp.wait()
        return carry

    lax.fori_loop(0, NU, drain, 0)


def write_out(*refs):
    sem = refs[8]
    copies = [pltpu.make_async_copy(refs[i], refs[4 + i], sem.at[i]) for i in range(4)]
    for cp in copies:
        cp.start()
    for cp in copies:
        cp.wait()


def per_device(tokens, cotangent, expert_ids, gate_scores, gate_weight, up_weight, down_weight):
    def sems(*shape):
        return pltpu.SemaphoreType.DMA(shape)

    anyspace = pl.BlockSpec(memory_space=pl.ANY)
    vmem = pl.BlockSpec(memory_space=pltpu.VMEM)
    scratch = [
        pltpu.VMEM((T, NP * C), BF),
        pltpu.VMEM((2, T, ND * C), BF),
        pltpu.VMEM((R, T), BF),
        pltpu.VMEM((T, R16), BF),
        pltpu.VMEM((T, R16), BF),
        pltpu.VMEM((T, R16), BF),
        pltpu.VMEM((T, 1), F32),
        pltpu.VMEM((T, 1), F32),
        pltpu.VMEM((NP, N, BLK, U), BF),
        pltpu.VMEM((2, ND, N, BLK, U), BF),
        pltpu.VMEM((2 * NA, N, BLK, U), BF),
        pltpu.VMEM((2, R, H), BF),
        pltpu.VMEM((4, H, HID), BF),
        pltpu.VMEM((2 * HID, H), BF),
        pltpu.VMEM((R, 4 * HID), F32),
        pltpu.VMEM((R, 2 * HID), F32),
        pltpu.VMEM((R, 4 * HID), F32),
        pltpu.VMEM((R, 2 * HID), F32),
        pltpu.VMEM((R, 2 * HID), BF),
        pltpu.VMEM((R, 4 * HID), BF),
        pltpu.VMEM((NU, 2, N, BLK, U), BF),
        pltpu.VMEM((NU, N, BLK, U), BF),
        pltpu.VMEM((NU, N, BLK, U), BF),
        pltpu.VMEM((NU, N, BLK, U), BF),
        pltpu.VMEM((NU, T, C), BF),
        pltpu.VMEM((NU, T, C), BF),
        pltpu.VMEM((NU, 2, T, C), BF),
        pltpu.VMEM((4, H, HID), BF),
        pltpu.VMEM((2 * HID, H), BF),
        pltpu.SemaphoreType.DMA, sems(2), sems(3), sems(3), sems(3),
        sems(NP), sems(NP), sems(2, ND), sems(2, ND), sems(NP), sems(NP), sems(NP, 2), sems(NP, 2),
        sems(2, R // RB), sems(2, R // RB),
        sems(NU), sems(NU), sems(NU), sems(NU), sems(NU), sems(NU), sems(NU), sems(NU),
        sems(NU, 2), sems(NU, 2), sems(NU, 2),
        sems(NU, 3), sems(NU, 3), sems(NU, 3),
    ]
    shapes = [((T, D), BF), ((1, D, HID), BF), ((1, D, HID), BF), ((1, HID, D), BF)]
    held = pl.pallas_call(
        body,
        out_shape=[pltpu.VMEM(*shape) for shape in shapes],
        in_specs=[anyspace, anyspace, vmem, vmem, anyspace, anyspace, anyspace],
        out_specs=[anyspace] * 4,
        scratch_shapes=scratch,
        compiler_params=pltpu.CompilerParams(
            collective_id=0, has_side_effects=True, vmem_limit_bytes=47 * 1024 * 1024
        ),
        cost_estimate=pl.CostEstimate(flops=6_000_000_000, bytes_accessed=20_000_000, transcendentals=100_000),
    )(tokens, cotangent, expert_ids.T, gate_scores.T, gate_weight, up_weight, down_weight)
    held = [pltpu.with_memory_space_constraint(h, pltpu.VMEM) for h in held]
    return tuple(
        pl.pallas_call(
            write_out,
            out_shape=[jax.ShapeDtypeStruct(*shape) for shape in shapes],
            in_specs=[anyspace] * 4,
            out_specs=[anyspace] * 4,
            scratch_shapes=[sems(4)],
            compiler_params=pltpu.CompilerParams(vmem_limit_bytes=2 * 1024 * 1024),
        )(*held)
    )


def solution(mesh):
    placed = (
        P("ep", None),
        P("ep", None),
        P("ep", None),
        P("ep", None),
        P("ep", None, "grp"),
        P("ep", None, "grp"),
        P("ep", "grp", None),
    )
    return jax.shard_map(
        per_device,
        mesh=mesh,
        in_specs=placed,
        out_specs=(P("ep", None), P("ep", None, "grp"), P("ep", None, "grp"), P("ep", "grp", None)),
        check_vma=False,
    )
```

```python
import functools

import jax
import jax.numpy as jnp
from jax import lax
from jax.experimental import pallas as pl
from jax.experimental.pallas import tpu as pltpu
from jax.sharding import PartitionSpec as P

BF = jnp.bfloat16
F32 = jnp.float32
MESH = pl.DeviceIdType.MESH

N = 16
SIDE = 4
T = 256
HID = 128
D = 7168
H = D // 2
W = 512
U = 128
C = 2 * U
NU = H // W
NA = H // C
NP = 5
ND = 6
R16 = N * 16
R8 = N * 8
R = R16 + R8
BLK = 48
OFFS = (
    (2, 2), (2, 3), (3, 2), (2, 1), (1, 2), (2, 0), (0, 2), (3, 1),
    (1, 3), (3, 3), (1, 1), (3, 0), (0, 3), (1, 0), (0, 1),
)
RB = 128
LAG = 4


def mm(a, b, ca=1, cb=0):
    return lax.dot_general(a, b, (((ca,), (cb,)), ((), ())), preferred_element_type=F32)


def pack(dst, g):
    g16 = g[:R16].reshape(N, 16, C)
    dst[:, 0:16, :] = g16[:, :, :U].astype(BF)
    dst[:, 16:32, :] = g16[:, :, U:].astype(BF)
    g8 = g[R16:].reshape(N, 8, C)
    dst[:, 32:48, :] = jnp.concatenate([g8[:, :, :U], g8[:, :, U:]], axis=1).astype(BF)


def body(
    tok, cot, ids, gs, gw, uw, dw,
    o_tok, o_gate, o_up, o_down,
    tokv, tokd, pm, q16, q8a, q8b, scale, gate_col,
    send_a, send_d, recv_a, xm, wgu, wd, acc_gu, acc_h, accr_gu, accr_h, hid, g2,
    pk, rsb, send_c, recv_c, zp, zr, fin, dwgu, dwd,
    tok_sem, tokd_sem, w_sem, ws_sem, wr_sem, as_sem, ar_sem, ds_a_sem, dr_a_sem, z1s_sem, z1r_sem, z2s_sem, z2r_sem,
    bs_sem, br_sem, ps_sem, pr_sem, cs_sem, cr_sem, xs_sem, xr_sem, gs_sem, gr_sem,
    ol_sem, os_sem, or_sem, dl_sem, ds_sem, dr_sem,
):
    g = lax.axis_index("grp")
    e = lax.axis_index("ep")
    z, c = g // 2, g % 2
    x, y = e // SIDE, e % SIDE
    other = 1 - c
    npc = NP - c
    ndc = NA - 2 * npc
    za = z + 1 - 2 * (z % 2)
    zb = 3 - z
    zo = 3 - za
    sib = (2 * z + other, e)

    def first(i):
        return za + (zb - za) * ((i + c) % 2)

    def second(i):
        return zb + (za - zb) * ((i + c) % 2)

    def at_z(zz):
        return (2 * zz + c, e)

    def peer(k):
        dx, dy = OFFS[k]
        if dx != dy:
            dx, dy = dx * other + dy * c, dy * other + dx * c
        return ((x + dx) % SIDE) * SIDE + (y + dy) % SIDE

    def remote(src, dst, ss, rs, dev):
        return pltpu.make_async_remote_copy(
            src_ref=src, dst_ref=dst, send_sem=ss, recv_sem=rs, device_id=dev, device_id_type=MESH
        )

    def mult(v, m):
        return pl.multiple_of(v, m)

    bar = pltpu.get_barrier_semaphore()
    for k in range(N - 1):
        pl.semaphore_signal(bar, inc=1, device_id=(g, peer(k)), device_id_type=MESH)
    for dev in (at_z(za), at_z(zb), sib):
        pl.semaphore_signal(bar, inc=1, device_id=dev, device_id_type=MESH)

    def load(src):
        col = mult(c * H + (z % 2) * npc * C, C)
        return pltpu.make_async_copy(src.at[:, pl.ds(col, NP * C)], tokv, tok_sem)

    def load_d(a):
        col = mult(c * H + 2 * npc * C, C)
        return pltpu.make_async_copy((tok, cot)[a].at[:, pl.ds(col, ND * C)], tokd.at[a], tokd_sem.at[a])

    @pl.when(z < 2)
    def _():
        load(tok).start()

    @pl.when(z >= 2)
    def _():
        load(cot).start()

    for a in range(2):
        load_d(a).start()

    my_half = mult(c * H, H)
    own_w = [
        pltpu.make_async_copy(gw.at[0, pl.ds(my_half, H)], wgu.at[c], w_sem.at[0]),
        pltpu.make_async_copy(uw.at[0, pl.ds(my_half, H)], wgu.at[2 + c], w_sem.at[1]),
        pltpu.make_async_copy(
            dw.at[0, :, pl.ds(my_half, H)], wd.at[pl.ds(mult(c * HID, HID), HID)], w_sem.at[2]
        ),
    ]
    for cp in own_w:
        cp.start()

    def column(row):
        return jnp.transpose(jnp.broadcast_to(row, (128, T)))[:, 0:1]

    idf = ids[...].astype(F32)
    e_row = jnp.min(idf, axis=0, keepdims=True)
    e_col = column(e_row)
    sub = lax.broadcasted_iota(jnp.int32, (T, T), 0)
    lane = lax.broadcasted_iota(jnp.int32, (T, T), 1)
    before = jnp.where(sub < lane, jnp.where(e_col == e_row, 1.0, 0.0), 0.0)
    rank_row = jnp.sum(before, axis=0, keepdims=True)
    valid = e_row < N
    slot16 = jnp.where(valid & (rank_row < 16), e_row * 16 + rank_row, -1.0)
    slot8 = jnp.where(valid & (rank_row >= 16), e_row * 8 + (rank_row - 16), -1.0)

    def onehot(test):
        return jnp.where(test, 1.0, 0.0).astype(BF)

    subf = sub.astype(F32)
    pm[:R16, :] = onehot(subf == slot16)
    pm[R16:, :] = onehot(subf[:R8] == slot8)
    gate_row = jnp.sum(jnp.where(idf < N, gs[...], 0.0), axis=0, keepdims=True)
    gate_col[...] = column(gate_row)
    scale[...] = column(jnp.where(z < 2, jnp.ones_like(gate_row), gate_row))

    pl.semaphore_wait(bar, N - 1 + 3)

    their_half = mult(other * H, H)
    sib_w = [
        remote(gw.at[0, pl.ds(their_half, H)], wgu.at[c], ws_sem.at[0], wr_sem.at[0], sib),
        remote(uw.at[0, pl.ds(their_half, H)], wgu.at[2 + c], ws_sem.at[1], wr_sem.at[1], sib),
        remote(
            dw.at[0, :, pl.ds(their_half, H)],
            wd.at[pl.ds(mult(c * HID, HID), HID)],
            ws_sem.at[2], wr_sem.at[2], sib,
        ),
    ]

    def spread(buf, n, ss, rs):
        recv_a[n, e] = buf[e]
        for k in range(N - 1):
            dst = peer(k)
            remote(buf.at[dst], recv_a.at[n, e], ss, rs, (g, dst)).start()

    def part_of(owner, i):
        return (owner // 2) * NA + (owner % 2) * npc + i

    def dispatch(i, carry):
        src = tokv[:, pl.ds(mult(i * C, C), C)]
        src = (scale[...] * src.astype(F32)).astype(BF)
        pack(send_a.at[i], mm(pm[...], src))
        spread(send_a.at[i], part_of(z, i), as_sem.at[i], ar_sem.at[i])
        return carry

    def dispatch_d(d, carry=0):
        for a in range(2):
            src = tokd[a, :, pl.ds(mult(d * C, C), C)]
            if a == 1:
                src = (gate_col[...] * src.astype(F32)).astype(BF)
            pack(send_d.at[a, d], mm(pm[...], src))
            spread(send_d.at[a, d], a * NA + 2 * npc + d, ds_a_sem.at[a, d], dr_a_sem.at[a, d])
        return carry

    load(tok).wait()
    lax.fori_loop(0, npc, dispatch, 0)
    for cp in sib_w:
        cp.start()
    for a in range(2):
        load_d(a).wait()

    lanef = lane.astype(F32)
    q16[...] = onehot(lanef == column(slot16))
    late_a = jnp.where(valid & (rank_row >= 16), e_row * 16 + (rank_row - 16), -16.0)
    q8a[...] = onehot(lanef == column(late_a))
    q8b[...] = onehot(lanef == column(late_a + 8))
    acc_gu[...] = jnp.zeros_like(acc_gu)
    acc_h[...] = jnp.zeros_like(acc_h)

    def arrived(i):
        blocks = recv_a.at[part_of(z, i), pl.ds(0, N - 1)]
        return remote(blocks, blocks, as_sem.at[i], ar_sem.at[i], sib)

    def arrived_d(a, d):
        blocks = recv_a.at[a * NA + 2 * npc + d, pl.ds(0, N - 1)]
        return remote(blocks, blocks, ds_a_sem.at[a, d], dr_a_sem.at[a, d], sib)

    def unpack(a, m):
        r = recv_a[a * NA + m]
        late8 = r[:, 32:48, :].astype(F32)
        left, right = pl.ds(mult(m * C, U), U), pl.ds(mult(m * C + U, U), U)
        xm[a, :R16, left] = r[:, 0:16, :].reshape(R16, U)
        xm[a, R16:, left] = late8[:, 0:8, :].reshape(R8, U).astype(BF)
        xm[a, :R16, right] = r[:, 16:32, :].reshape(R16, U)
        xm[a, R16:, right] = late8[:, 8:16, :].reshape(R8, U).astype(BF)

    def multiply(a, m):
        cols = pl.ds(mult(m * C, C), C)
        if a == 0:
            w = jnp.concatenate([wgu[k, cols, :] for k in range(4)], axis=1)
            acc_gu[...] += mm(xm[0, :, cols], w)
        else:
            acc_h[...] += mm(xm[1, :, cols], wd[:, cols], 1, 1)

    def process_of(owner, i):
        a, m = owner // 2, (owner % 2) * npc + i
        unpack(a, m)

        @pl.when(a == 0)
        def _():
            multiply(0, m)

        @pl.when(a == 1)
        def _():
            multiply(1, m)

    def process_d(d):
        for a in range(2):
            arrived_d(a, d).wait_recv()
            unpack(a, 2 * npc + d)
            multiply(a, 2 * npc + d)

    def step1(i):
        blk = recv_a.at[part_of(z, i)]
        return remote(blk, blk, z1s_sem.at[i], z1r_sem.at[i], at_z(first(i)))

    def step2(i, fwd):
        blk = recv_a.at[part_of(first(i), i) if fwd else part_of(z, i)]
        return remote(blk, blk, z2s_sem.at[i, fwd], z2r_sem.at[i, fwd], at_z(second(i)))

    dispatch_d(0)

    def gather1(i, carry):
        arrived(i).wait_recv()
        step1(i).start()
        step2(i, 0).start()

        @pl.when(i + 1 < ndc)
        def _():
            dispatch_d(i + 1)

        return carry

    lax.fori_loop(0, npc, gather1, 0)
    lax.fori_loop(npc + 1, ndc, dispatch_d, 0)
    for k in range(3):
        own_w[k].wait()
        sib_w[k].wait_recv()

    def gather2(i, carry):
        step1(i).wait_recv()
        step2(i, 1).start()
        process_of(z, i)
        process_of(first(i), i)

        @pl.when((i >= 1) & (i < ndc + 1))
        def _():
            process_d(i - 1)

        return carry

    lax.fori_loop(0, npc, gather2, 0)

    def gather3(i, carry):
        @pl.when(i + npc - 1 < ndc)
        def _():
            process_d(i + npc - 1)

        step2(i, 0).wait_recv()
        process_of(second(i), i)
        step2(i, 1).wait_recv()
        process_of(zo, i)
        return carry

    lax.fori_loop(0, npc, gather3, 0)

    def swap(i):
        rows = pl.ds(mult(i * RB, RB), RB)
        return (
            remote(acc_gu.at[rows], accr_gu.at[rows], bs_sem.at[0, i], br_sem.at[0, i], sib),
            remote(acc_h.at[rows], accr_h.at[rows], bs_sem.at[1, i], br_sem.at[1, i], sib),
        )

    for i in range(R // RB):
        for cp in swap(i):
            cp.start()

    def act(i, carry):
        rows = pl.ds(mult(i * RB, RB), RB)
        for cp in swap(i):
            cp.wait_recv()
        gu = acc_gu[rows, :] + accr_gu[rows, :]
        gh = acc_h[rows, :] + accr_h[rows, :]
        gp, up = gu[:, : 2 * HID], gu[:, 2 * HID :]
        sg = jax.nn.sigmoid(gp)
        silu = gp * sg
        hid[rows, :] = (silu * up).astype(BF)
        g2[rows, : 2 * HID] = (gh * up * sg * (1.0 + gp * (1.0 - sg))).astype(BF)
        g2[rows, 2 * HID :] = (gh * silu).astype(BF)
        return carry

    lax.fori_loop(0, R // RB, act, 0)

    def half(j):
        b = ((z + 1) // 2) % 2
        return b + (z // 2 - b) * ((j + c) % 2)

    def pair(j):
        return remote(pk.at[j, 1 - half(j)], rsb.at[j], ps_sem.at[j], pr_sem.at[j], at_z(first(j)))

    def row_grad(j, carry):
        cols = pl.ds(mult(j * W, W), W)
        w = jnp.concatenate([wgu[i, cols, :] for i in range(4)], axis=1)
        r = mm(g2[...], w, 1, 1)
        for h in range(2):
            pack(pk.at[j, h], r[:, h * C : (h + 1) * C])
        pair(j).start()
        return carry

    lax.fori_loop(0, NU, row_grad, 0)

    def back(j, carry):
        pair(j).wait_recv()
        send_c[j] = (pk[j, half(j)].astype(F32) + rsb[j].astype(F32)).astype(BF)
        recv_c[j, e] = send_c[j, e]
        for k in range(N - 1):
            dst = peer(k)
            remote(send_c.at[j, dst], recv_c.at[j, e], cs_sem.at[j], cr_sem.at[j], (g, dst)).start()
        return carry

    lax.fori_loop(0, NU, back, 0)

    def cross(j):
        return remote(zp.at[j], zr.at[j], xs_sem.at[j], xr_sem.at[j], at_z(second(j)))

    def whole(j):
        blk = fin.at[j, half(j)]
        return remote(blk, blk, gs_sem.at[j], gr_sem.at[j], at_z(first(j)))

    def out_cols(j, p):
        return pl.ds(mult(c * H + j * W + p * C, C), C)

    def out_local(j, p):
        return pltpu.make_async_copy(fin.at[j, p], o_tok.at[:, out_cols(j, p)], ol_sem.at[j, p])

    def out_sib(j, p):
        return remote(fin.at[j, p], o_tok.at[:, out_cols(j, p)], os_sem.at[j, p], or_sem.at[j, p], sib)

    def grads_out(j):
        rows = pl.ds(mult(j * W, W), W)
        orow = pl.ds(mult(c * H + j * W, W), W)
        local, far = [], []
        for i, out in enumerate((o_gate, o_up)):
            local.append(pltpu.make_async_copy(dwgu.at[2 * i + c, rows], out.at[0, orow], dl_sem.at[j, i]))
            far.append(remote(dwgu.at[2 * i + other, rows], out.at[0, orow], ds_sem.at[j, i], dr_sem.at[j, i], sib))
        mine, yours = pl.ds(mult(c * HID, HID), HID), pl.ds(mult(other * HID, HID), HID)
        local.append(pltpu.make_async_copy(dwd.at[mine, rows], o_down.at[0, :, orow], dl_sem.at[j, 2]))
        far.append(remote(dwd.at[yours, rows], o_down.at[0, :, orow], ds_sem.at[j, 2], dr_sem.at[j, 2], sib))
        return local, far

    def pipe(t, carry):
        @pl.when(t < NU)
        def _():
            blocks = recv_c.at[t, pl.ds(0, N - 1)]
            remote(blocks, blocks, cs_sem.at[t], cr_sem.at[t], sib).wait_recv()
            r = recv_c[t]
            r8 = r[:, 32:48, :].reshape(R16, U)
            for p in range(2):
                r16 = r[:, 16 * p : 16 * p + 16, :].reshape(R16, U)
                zp[t, :, p * U : (p + 1) * U] = (mm(q16[...], r16) + mm((q8a, q8b)[p][...], r8)).astype(BF)
            cross(t).start()

        @pl.when((t >= LAG) & (t < NU + LAG))
        def _():
            j = t - LAG
            cross(j).wait_recv()
            fin[j, half(j)] = (zp[j].astype(F32) + zr[j].astype(F32)).astype(BF)
            whole(j).start()

        @pl.when(t >= 2 * LAG)
        def _():
            whole(t - 2 * LAG).wait_recv()
            for p in range(2):
                out_local(t - 2 * LAG, p).start()
                out_sib(t - 2 * LAG, p).start()

        @pl.when(t < NU)
        def _():
            cols = pl.ds(mult(t * W, W), W)
            d1 = mm(xm[0, :, cols], g2[...], 0, 0)
            for i in range(4):
                dwgu[i, cols, :] = d1[:, i * HID : (i + 1) * HID].astype(BF)
            dwd[:, cols] = mm(hid[...], xm[1, :, cols], 0, 0).astype(BF)
            local, far = grads_out(t)
            for cp in local + far:
                cp.start()

        return carry

    lax.fori_loop(0, NU + 2 * LAG, pipe, 0)

    for i in range(3):
        sib_w[i].wait_send()
        for cp in swap(i):
            cp.wait_send()

    def drain_a(i, carry):
        arrived(i).wait_send()
        step1(i).wait_send()
        step2(i, 0).wait_send()
        step2(i, 1).wait_send()
        return carry

    lax.fori_loop(0, npc, drain_a, 0)

    def drain_d(d, carry):
        for a in range(2):
            arrived_d(a, d).wait_send()
        return carry

    lax.fori_loop(0, ndc, drain_d, 0)

    def drain(j, carry):
        blocks = send_c.at[j, pl.ds(0, N - 1)]
        remote(blocks, blocks, cs_sem.at[j], cr_sem.at[j], sib).wait_send()
        for cp in (pair(j), cross(j), whole(j)):
            cp.wait_send()
        for p in range(2):
            out_local(j, p).wait()
            out_sib(j, p).wait()
        local, far = grads_out(j)
        for cp in local + far:
            cp.wait()
        return carry

    lax.fori_loop(0, NU, drain, 0)


def write_out(*refs):
    sem = refs[8]
    copies = [pltpu.make_async_copy(refs[i], refs[4 + i], sem.at[i]) for i in range(4)]
    for cp in copies:
        cp.start()
    for cp in copies:
        cp.wait()


def per_device(tokens, cotangent, expert_ids, gate_scores, gate_weight, up_weight, down_weight):
    def sems(*shape):
        return pltpu.SemaphoreType.DMA(shape)

    anyspace = pl.BlockSpec(memory_space=pl.ANY)
    vmem = pl.BlockSpec(memory_space=pltpu.VMEM)
    scratch = [
        pltpu.VMEM((T, NP * C), BF),
        pltpu.VMEM((2, T, ND * C), BF),
        pltpu.VMEM((R, T), BF),
        pltpu.VMEM((T, R16), BF),
        pltpu.VMEM((T, R16), BF),
        pltpu.VMEM((T, R16), BF),
        pltpu.VMEM((T, 1), F32),
        pltpu.VMEM((T, 1), F32),
        pltpu.VMEM((NP, N, BLK, U), BF),
        pltpu.VMEM((2, ND, N, BLK, U), BF),
        pltpu.VMEM((2 * NA, N, BLK, U), BF),
        pltpu.VMEM((2, R, H), BF),
        pltpu.VMEM((4, H, HID), BF),
        pltpu.VMEM((2 * HID, H), BF),
        pltpu.VMEM((R, 4 * HID), F32),
        pltpu.VMEM((R, 2 * HID), F32),
        pltpu.VMEM((R, 4 * HID), F32),
        pltpu.VMEM((R, 2 * HID), F32),
        pltpu.VMEM((R, 2 * HID), BF),
        pltpu.VMEM((R, 4 * HID), BF),
        pltpu.VMEM((NU, 2, N, BLK, U), BF),
        pltpu.VMEM((NU, N, BLK, U), BF),
        pltpu.VMEM((NU, N, BLK, U), BF),
        pltpu.VMEM((NU, N, BLK, U), BF),
        pltpu.VMEM((NU, T, C), BF),
        pltpu.VMEM((NU, T, C), BF),
        pltpu.VMEM((NU, 2, T, C), BF),
        pltpu.VMEM((4, H, HID), BF),
        pltpu.VMEM((2 * HID, H), BF),
        pltpu.SemaphoreType.DMA, sems(2), sems(3), sems(3), sems(3),
        sems(NP), sems(NP), sems(2, ND), sems(2, ND), sems(NP), sems(NP), sems(NP, 2), sems(NP, 2),
        sems(2, R // RB), sems(2, R // RB),
        sems(NU), sems(NU), sems(NU), sems(NU), sems(NU), sems(NU), sems(NU), sems(NU),
        sems(NU, 2), sems(NU, 2), sems(NU, 2),
        sems(NU, 3), sems(NU, 3), sems(NU, 3),
    ]
    shapes = [((T, D), BF), ((1, D, HID), BF), ((1, D, HID), BF), ((1, HID, D), BF)]
    held = pl.pallas_call(
        body,
        out_shape=[pltpu.VMEM(*shape) for shape in shapes],
        in_specs=[anyspace, anyspace, vmem, vmem, anyspace, anyspace, anyspace],
        out_specs=[anyspace] * 4,
        scratch_shapes=scratch,
        compiler_params=pltpu.CompilerParams(
            collective_id=0, has_side_effects=True, vmem_limit_bytes=47 * 1024 * 1024
        ),
        cost_estimate=pl.CostEstimate(flops=6_000_000_000, bytes_accessed=20_000_000, transcendentals=100_000),
    )(tokens, cotangent, expert_ids.T, gate_scores.T, gate_weight, up_weight, down_weight)
    held = [pltpu.with_memory_space_constraint(h, pltpu.VMEM) for h in held]
    return tuple(
        pl.pallas_call(
            write_out,
            out_shape=[jax.ShapeDtypeStruct(*shape) for shape in shapes],
            in_specs=[anyspace] * 4,
            out_specs=[anyspace] * 4,
            scratch_shapes=[sems(4)],
            compiler_params=pltpu.CompilerParams(vmem_limit_bytes=2 * 1024 * 1024),
        )(*held)
    )


def solution(mesh):
    placed = (
        P("ep", None),
        P("ep", None),
        P("ep", None),
        P("ep", None),
        P("ep", None, "grp"),
        P("ep", None, "grp"),
        P("ep", "grp", None),
    )
    return jax.shard_map(
        per_device,
        mesh=mesh,
        in_specs=placed,
        out_specs=(P("ep", None), P("ep", None, "grp"), P("ep", None, "grp"), P("ep", "grp", None)),
        check_vma=False,
    )
```

```python
import functools

import jax
import jax.numpy as jnp
from jax import lax
from jax.experimental import pallas as pl
from jax.experimental.pallas import tpu as pltpu
from jax.sharding import PartitionSpec as P

BF = jnp.bfloat16
F32 = jnp.float32
MESH = pl.DeviceIdType.MESH

N = 16
SIDE = 4
T = 256
HID = 128
D = 7168
H = D // 2
W = 512
U = 128
C = 2 * U
NU = H // W
NA = H // C
NP = 5
ND = 6
R16 = N * 16
R8 = N * 8
R = R16 + R8
BLK = 48
OFFS = (
    (2, 2), (2, 3), (3, 2), (2, 1), (1, 2), (2, 0), (0, 2), (3, 1),
    (1, 3), (3, 3), (1, 1), (3, 0), (0, 3), (1, 0), (0, 1),
)
RB = 128
LAG = 4
GL = 3
N1 = 2


def mm(a, b, ca=1, cb=0):
    return lax.dot_general(a, b, (((ca,), (cb,)), ((), ())), preferred_element_type=F32)


def pack(dst, g):
    g16 = g[:R16].reshape(N, 16, C)
    dst[:, 0:16, :] = g16[:, :, :U].astype(BF)
    dst[:, 16:32, :] = g16[:, :, U:].astype(BF)
    g8 = g[R16:].reshape(N, 8, C)
    dst[:, 32:48, :] = jnp.concatenate([g8[:, :, :U], g8[:, :, U:]], axis=1).astype(BF)


def body(
    tok, cot, ids, gs, gw, uw, dw,
    o_tok, o_gate, o_up, o_down,
    tokv, tokd, pm, q16, q8a, q8b, scale, gate_col,
    send_a, send_d, recv_a, xm, wgu, wd, acc_gu, acc_h, accr_gu, accr_h, hid, g2,
    pk, rsb, send_c, recv_c, recv_i, zx, zy, zp, zr, fin, dwgu, dwd,
    tok_sem, tokd_sem, w_sem, ws_sem, wr_sem, as_sem, ar_sem, ds_a_sem, dr_a_sem, z1s_sem, z1r_sem, z2s_sem, z2r_sem,
    bs_sem, br_sem, ps_sem, pr_sem, cs_sem, cr_sem, xs_sem, xr_sem, gs_sem, gr_sem,
    is_sem, ir_sem, ts_sem, tr_sem,
    ol_sem, os_sem, or_sem, dl_sem, ds_sem, dr_sem,
):
    g = lax.axis_index("grp")
    e = lax.axis_index("ep")
    z, c = g // 2, g % 2
    x, y = e // SIDE, e % SIDE
    other = 1 - c
    npc = NP - c
    ndc = NA - 2 * npc
    za = z + 1 - 2 * (z % 2)
    zb = 3 - z
    zo = 3 - za
    sib = (2 * z + other, e)

    def first(i):
        return za + (zb - za) * ((i + c) % 2)

    def second(i):
        return zb + (za - zb) * ((i + c) % 2)

    def at_z(zz):
        return (2 * zz + c, e)

    def peer(k):
        dx, dy = OFFS[k]
        if dx != dy:
            dx, dy = dx * other + dy * c, dy * other + dx * c
        return ((x + dx) % SIDE) * SIDE + (y + dy) % SIDE

    def remote(src, dst, ss, rs, dev):
        return pltpu.make_async_remote_copy(
            src_ref=src, dst_ref=dst, send_sem=ss, recv_sem=rs, device_id=dev, device_id_type=MESH
        )

    def mult(v, m):
        return pl.multiple_of(v, m)

    bar = pltpu.get_barrier_semaphore()
    for k in range(N - 1):
        pl.semaphore_signal(bar, inc=1, device_id=(g, peer(k)), device_id_type=MESH)
    for dev in (at_z(za), at_z(zb), sib):
        pl.semaphore_signal(bar, inc=1, device_id=dev, device_id_type=MESH)

    def load(src):
        col = mult(c * H + (z % 2) * npc * C, C)
        return pltpu.make_async_copy(src.at[:, pl.ds(col, NP * C)], tokv, tok_sem)

    def load_d(a):
        col = mult(c * H + 2 * npc * C, C)
        return pltpu.make_async_copy((tok, cot)[a].at[:, pl.ds(col, ND * C)], tokd.at[a], tokd_sem.at[a])

    @pl.when(z < 2)
    def _():
        load(tok).start()

    @pl.when(z >= 2)
    def _():
        load(cot).start()

    for a in range(2):
        load_d(a).start()

    my_half = mult(c * H, H)
    own_w = [
        pltpu.make_async_copy(gw.at[0, pl.ds(my_half, H)], wgu.at[c], w_sem.at[0]),
        pltpu.make_async_copy(uw.at[0, pl.ds(my_half, H)], wgu.at[2 + c], w_sem.at[1]),
        pltpu.make_async_copy(
            dw.at[0, :, pl.ds(my_half, H)], wd.at[pl.ds(mult(c * HID, HID), HID)], w_sem.at[2]
        ),
    ]
    for cp in own_w:
        cp.start()

    def column(row):
        return jnp.transpose(jnp.broadcast_to(row, (128, T)))[:, 0:1]

    idf = ids[...].astype(F32)
    e_row = jnp.min(idf, axis=0, keepdims=True)
    e_col = column(e_row)
    sub = lax.broadcasted_iota(jnp.int32, (T, T), 0)
    lane = lax.broadcasted_iota(jnp.int32, (T, T), 1)
    before = jnp.where(sub < lane, jnp.where(e_col == e_row, 1.0, 0.0), 0.0)
    rank_row = jnp.sum(before, axis=0, keepdims=True)
    valid = e_row < N
    slot16 = jnp.where(valid & (rank_row < 16), e_row * 16 + rank_row, -1.0)
    slot8 = jnp.where(valid & (rank_row >= 16), e_row * 8 + (rank_row - 16), -1.0)

    def onehot(test):
        return jnp.where(test, 1.0, 0.0).astype(BF)

    subf = sub.astype(F32)
    pm[:R16, :] = onehot(subf == slot16)
    pm[R16:, :] = onehot(subf[:R8] == slot8)
    gate_row = jnp.sum(jnp.where(idf < N, gs[...], 0.0), axis=0, keepdims=True)
    gate_col[...] = column(gate_row)
    scale[...] = column(jnp.where(z < 2, jnp.ones_like(gate_row), gate_row))

    pl.semaphore_wait(bar, N - 1 + 3)

    their_half = mult(other * H, H)
    sib_w = [
        remote(gw.at[0, pl.ds(their_half, H)], wgu.at[c], ws_sem.at[0], wr_sem.at[0], sib),
        remote(uw.at[0, pl.ds(their_half, H)], wgu.at[2 + c], ws_sem.at[1], wr_sem.at[1], sib),
        remote(
            dw.at[0, :, pl.ds(their_half, H)],
            wd.at[pl.ds(mult(c * HID, HID), HID)],
            ws_sem.at[2], wr_sem.at[2], sib,
        ),
    ]

    def spread(buf, n, ss, rs):
        recv_a[n, e] = buf[e]
        for k in range(N - 1):
            dst = peer(k)
            remote(buf.at[dst], recv_a.at[n, e], ss, rs, (g, dst)).start()

    def part_of(owner, i):
        return (owner // 2) * NA + (owner % 2) * npc + i

    def dispatch(i, carry):
        src = tokv[:, pl.ds(mult(i * C, C), C)]
        src = (scale[...] * src.astype(F32)).astype(BF)
        pack(send_a.at[i], mm(pm[...], src))
        spread(send_a.at[i], part_of(z, i), as_sem.at[i], ar_sem.at[i])
        return carry

    def dispatch_d(d, carry=0):
        for a in range(2):
            src = tokd[a, :, pl.ds(mult(d * C, C), C)]
            if a == 1:
                src = (gate_col[...] * src.astype(F32)).astype(BF)
            pack(send_d.at[a, d], mm(pm[...], src))
            spread(send_d.at[a, d], a * NA + 2 * npc + d, ds_a_sem.at[a, d], dr_a_sem.at[a, d])
        return carry

    load(tok).wait()
    lax.fori_loop(0, npc, dispatch, 0)
    for cp in sib_w:
        cp.start()
    for a in range(2):
        load_d(a).wait()

    lanef = lane.astype(F32)
    q16[...] = onehot(lanef == column(slot16))
    late_a = jnp.where(valid & (rank_row >= 16), e_row * 16 + (rank_row - 16), -16.0)
    q8a[...] = onehot(lanef == column(late_a))
    q8b[...] = onehot(lanef == column(late_a + 8))
    acc_gu[...] = jnp.zeros_like(acc_gu)
    acc_h[...] = jnp.zeros_like(acc_h)

    def arrived(i):
        blocks = recv_a.at[part_of(z, i), pl.ds(0, N - 1)]
        return remote(blocks, blocks, as_sem.at[i], ar_sem.at[i], sib)

    def arrived_d(a, d):
        blocks = recv_a.at[a * NA + 2 * npc + d, pl.ds(0, N - 1)]
        return remote(blocks, blocks, ds_a_sem.at[a, d], dr_a_sem.at[a, d], sib)

    def unpack(a, m):
        r = recv_a[a * NA + m]
        late8 = r[:, 32:48, :].astype(F32)
        left, right = pl.ds(mult(m * C, U), U), pl.ds(mult(m * C + U, U), U)
        xm[a, :R16, left] = r[:, 0:16, :].reshape(R16, U)
        xm[a, R16:, left] = late8[:, 0:8, :].reshape(R8, U).astype(BF)
        xm[a, :R16, right] = r[:, 16:32, :].reshape(R16, U)
        xm[a, R16:, right] = late8[:, 8:16, :].reshape(R8, U).astype(BF)

    def multiply(a, m):
        cols = pl.ds(mult(m * C, C), C)
        if a == 0:
            w = jnp.concatenate([wgu[k, cols, :] for k in range(4)], axis=1)
            acc_gu[...] += mm(xm[0, :, cols], w)
        else:
            acc_h[...] += mm(xm[1, :, cols], wd[:, cols], 1, 1)

    def process_of(owner, i):
        a, m = owner // 2, (owner % 2) * npc + i
        unpack(a, m)

        @pl.when(a == 0)
        def _():
            multiply(0, m)

        @pl.when(a == 1)
        def _():
            multiply(1, m)

    def process_d(d):
        for a in range(2):
            arrived_d(a, d).wait_recv()
            unpack(a, 2 * npc + d)
            multiply(a, 2 * npc + d)

    def step1(i):
        blk = recv_a.at[part_of(z, i)]
        return remote(blk, blk, z1s_sem.at[i], z1r_sem.at[i], at_z(first(i)))

    def step2(i, fwd):
        blk = recv_a.at[part_of(first(i), i) if fwd else part_of(z, i)]
        return remote(blk, blk, z2s_sem.at[i, fwd], z2r_sem.at[i, fwd], at_z(second(i)))

    dispatch_d(0)

    def gather1(i, carry):
        arrived(i).wait_recv()
        step1(i).start()
        step2(i, 0).start()

        @pl.when(i + 1 < ndc)
        def _():
            dispatch_d(i + 1)

        return carry

    lax.fori_loop(0, npc, gather1, 0)
    lax.fori_loop(npc + 1, ndc, dispatch_d, 0)
    for k in range(3):
        own_w[k].wait()
        sib_w[k].wait_recv()

    def gather2(i, carry):
        step1(i).wait_recv()
        step2(i, 1).start()
        process_of(z, i)
        process_of(first(i), i)

        @pl.when((i >= 1) & (i < ndc + 1))
        def _():
            process_d(i - 1)

        return carry

    lax.fori_loop(0, npc, gather2, 0)

    def gather3(i, carry):
        @pl.when(i + npc - 1 < ndc)
        def _():
            process_d(i + npc - 1)

        step2(i, 0).wait_recv()
        process_of(second(i), i)
        step2(i, 1).wait_recv()
        process_of(zo, i)
        return carry

    lax.fori_loop(0, npc, gather3, 0)

    def swap(i):
        rows = pl.ds(mult(i * RB, RB), RB)
        return (
            remote(acc_gu.at[rows], accr_gu.at[rows], bs_sem.at[0, i], br_sem.at[0, i], sib),
            remote(acc_h.at[rows], accr_h.at[rows], bs_sem.at[1, i], br_sem.at[1, i], sib),
        )

    for i in range(R // RB):
        for cp in swap(i):
            cp.start()

    def act(i, carry):
        rows = pl.ds(mult(i * RB, RB), RB)
        for cp in swap(i):
            cp.wait_recv()
        gu = acc_gu[rows, :] + accr_gu[rows, :]
        gh = acc_h[rows, :] + accr_h[rows, :]
        gp, up = gu[:, : 2 * HID], gu[:, 2 * HID :]
        sg = jax.nn.sigmoid(gp)
        silu = gp * sg
        hid[rows, :] = (silu * up).astype(BF)
        g2[rows, : 2 * HID] = (gh * up * sg * (1.0 + gp * (1.0 - sg))).astype(BF)
        g2[rows, 2 * HID :] = (gh * silu).astype(BF)
        return carry

    lax.fori_loop(0, R // RB, act, 0)

    def half(j):
        b = ((z + 1) // 2) % 2
        return b + (z // 2 - b) * ((j + c) % 2)

    def pair(j):
        return remote(pk.at[j, 1 - half(j)], rsb.at[j], ps_sem.at[j], pr_sem.at[j], at_z(first(j)))

    def row_grad(j):
        cols = pl.ds(mult(j * W, W), W)
        w = jnp.concatenate([wgu[i, cols, :] for i in range(4)], axis=1)
        r = mm(g2[...], w, 1, 1)
        for h in range(2):
            pack(pk.at[j, h], r[:, h * C : (h + 1) * C])

    def early(j, carry):
        row_grad(j)
        for h in range(2):
            recv_i[j, h, e] = pk[j, h, e]
            for k in range(N - 1):
                dst = peer(k)
                remote(
                    pk.at[j, h, dst], recv_i.at[j, h, e], is_sem.at[j, h], ir_sem.at[j, h], (g, dst)
                ).start()
        return carry

    def summed(j, carry):
        row_grad(j)
        pair(j).start()
        return carry

    lax.fori_loop(0, 1, early, 0)
    lax.fori_loop(N1, NU, summed, 0)
    lax.fori_loop(1, N1, early, 0)

    def back(j, carry):
        pair(j).wait_recv()
        send_c[j] = (pk[j, half(j)].astype(F32) + rsb[j].astype(F32)).astype(BF)
        recv_c[j, e] = send_c[j, e]
        for k in range(N - 1):
            dst = peer(k)
            remote(send_c.at[j, dst], recv_c.at[j, e], cs_sem.at[j], cr_sem.at[j], (g, dst)).start()
        return carry

    lax.fori_loop(N1, NU, back, 0)

    def early_all(j, h):
        blocks = recv_i.at[j, h, pl.ds(0, N - 1)]
        return remote(blocks, blocks, is_sem.at[j, h], ir_sem.at[j, h], sib)

    def give(j):
        return remote(zx.at[j], zy.at[j], ts_sem.at[j], tr_sem.at[j], at_z(first(j)))

    def cross(j):
        return remote(zp.at[j], zr.at[j], xs_sem.at[j], xr_sem.at[j], at_z(second(j)))

    def whole(j):
        blk = fin.at[j, half(j)]
        return remote(blk, blk, gs_sem.at[j], gr_sem.at[j], at_z(first(j)))

    def out_cols(j, p):
        return pl.ds(mult(c * H + j * W + p * C, C), C)

    def out_local(j, p):
        return pltpu.make_async_copy(fin.at[j, p], o_tok.at[:, out_cols(j, p)], ol_sem.at[j, p])

    def out_sib(j, p):
        return remote(fin.at[j, p], o_tok.at[:, out_cols(j, p)], os_sem.at[j, p], or_sem.at[j, p], sib)

    def grads_out(j):
        rows = pl.ds(mult(j * W, W), W)
        orow = pl.ds(mult(c * H + j * W, W), W)
        local, far = [], []
        for i, out in enumerate((o_gate, o_up)):
            local.append(pltpu.make_async_copy(dwgu.at[2 * i + c, rows], out.at[0, orow], dl_sem.at[j, i]))
            far.append(remote(dwgu.at[2 * i + other, rows], out.at[0, orow], ds_sem.at[j, i], dr_sem.at[j, i], sib))
        mine, yours = pl.ds(mult(c * HID, HID), HID), pl.ds(mult(other * HID, HID), HID)
        local.append(pltpu.make_async_copy(dwd.at[mine, rows], o_down.at[0, :, orow], dl_sem.at[j, 2]))
        far.append(remote(dwd.at[yours, rows], o_down.at[0, :, orow], ds_sem.at[j, 2], dr_sem.at[j, 2], sib))
        return local, far

    def scatter(r):
        r8 = r[:, 32:48, :].reshape(R16, U)
        parts = []
        for p in range(2):
            r16 = r[:, 16 * p : 16 * p + 16, :].reshape(R16, U)
            parts.append((mm(q16[...], r16) + mm((q8a, q8b)[p][...], r8)).astype(BF))
        return jnp.concatenate(parts, axis=1)

    def crossed(j):
        cross(j).wait_recv()
        fin[j, half(j)] = (zp[j].astype(F32) + zr[j].astype(F32)).astype(BF)
        whole(j).start()

    def finished(j):
        whole(j).wait_recv()
        for p in range(2):
            out_local(j, p).start()
            out_sib(j, p).start()

    def pipe(t, carry):
        @pl.when(t < N1)
        def _():
            for h in range(2):
                early_all(t, h).wait_recv()
            zx[t] = scatter(recv_i[t, 1 - half(t)])
            give(t).start()
            zp[t] = scatter(recv_i[t, half(t)])

        @pl.when((t >= N1) & (t < NU))
        def _():
            blocks = recv_c.at[t, pl.ds(0, N - 1)]
            remote(blocks, blocks, cs_sem.at[t], cr_sem.at[t], sib).wait_recv()
            zp[t] = scatter(recv_c[t])
            cross(t).start()

        @pl.when((t >= GL) & (t < N1 + GL))
        def _():
            j = t - GL
            give(j).wait_recv()
            zp[j] = (zp[j].astype(F32) + zy[j].astype(F32)).astype(BF)
            cross(j).start()

        @pl.when((t >= GL + LAG) & (t < N1 + GL + LAG))
        def _():
            crossed(t - GL - LAG)

        @pl.when((t >= N1 + LAG) & (t < NU + LAG))
        def _():
            crossed(t - LAG)

        @pl.when((t >= GL + 2 * LAG) & (t < N1 + GL + 2 * LAG))
        def _():
            finished(t - GL - 2 * LAG)

        @pl.when(t >= N1 + 2 * LAG)
        def _():
            finished(t - 2 * LAG)

        @pl.when(t < NU)
        def _():
            cols = pl.ds(mult(t * W, W), W)
            d1 = mm(xm[0, :, cols], g2[...], 0, 0)
            for i in range(4):
                dwgu[i, cols, :] = d1[:, i * HID : (i + 1) * HID].astype(BF)
            dwd[:, cols] = mm(hid[...], xm[1, :, cols], 0, 0).astype(BF)
            local, far = grads_out(t)
            for cp in local + far:
                cp.start()

        return carry

    lax.fori_loop(0, NU + 2 * LAG, pipe, 0)

    for i in range(3):
        sib_w[i].wait_send()
        for cp in swap(i):
            cp.wait_send()

    def drain_a(i, carry):
        arrived(i).wait_send()
        step1(i).wait_send()
        step2(i, 0).wait_send()
        step2(i, 1).wait_send()
        return carry

    lax.fori_loop(0, npc, drain_a, 0)

    def drain_d(d, carry):
        for a in range(2):
            arrived_d(a, d).wait_send()
        return carry

    lax.fori_loop(0, ndc, drain_d, 0)

    for j in range(N1):
        give(j).wait_send()
        for h in range(2):
            early_all(j, h).wait_send()

    def drain_c(j, carry):
        blocks = send_c.at[j, pl.ds(0, N - 1)]
        remote(blocks, blocks, cs_sem.at[j], cr_sem.at[j], sib).wait_send()
        pair(j).wait_send()
        return carry

    lax.fori_loop(N1, NU, drain_c, 0)

    def drain(j, carry):
        for cp in (cross(j), whole(j)):
            cp.wait_send()
        for p in range(2):
            out_local(j, p).wait()
            out_sib(j, p).wait()
        local, far = grads_out(j)
        for cp in local + far:
            cp.wait()
        return carry

    lax.fori_loop(0, NU, drain, 0)


def write_out(*refs):
    sem = refs[8]
    copies = [pltpu.make_async_copy(refs[i], refs[4 + i], sem.at[i]) for i in range(4)]
    for cp in copies:
        cp.start()
    for cp in copies:
        cp.wait()


def per_device(tokens, cotangent, expert_ids, gate_scores, gate_weight, up_weight, down_weight):
    def sems(*shape):
        return pltpu.SemaphoreType.DMA(shape)

    anyspace = pl.BlockSpec(memory_space=pl.ANY)
    vmem = pl.BlockSpec(memory_space=pltpu.VMEM)
    scratch = [
        pltpu.VMEM((T, NP * C), BF),
        pltpu.VMEM((2, T, ND * C), BF),
        pltpu.VMEM((R, T), BF),
        pltpu.VMEM((T, R16), BF),
        pltpu.VMEM((T, R16), BF),
        pltpu.VMEM((T, R16), BF),
        pltpu.VMEM((T, 1), F32),
        pltpu.VMEM((T, 1), F32),
        pltpu.VMEM((NP, N, BLK, U), BF),
        pltpu.VMEM((2, ND, N, BLK, U), BF),
        pltpu.VMEM((2 * NA, N, BLK, U), BF),
        pltpu.VMEM((2, R, H), BF),
        pltpu.VMEM((4, H, HID), BF),
        pltpu.VMEM((2 * HID, H), BF),
        pltpu.VMEM((R, 4 * HID), F32),
        pltpu.VMEM((R, 2 * HID), F32),
        pltpu.VMEM((R, 4 * HID), F32),
        pltpu.VMEM((R, 2 * HID), F32),
        pltpu.VMEM((R, 2 * HID), BF),
        pltpu.VMEM((R, 4 * HID), BF),
        pltpu.VMEM((NU, 2, N, BLK, U), BF),
        pltpu.VMEM((NU, N, BLK, U), BF),
        pltpu.VMEM((NU, N, BLK, U), BF),
        pltpu.VMEM((NU, N, BLK, U), BF),
        pltpu.VMEM((N1, 2, N, BLK, U), BF),
        pltpu.VMEM((N1, T, C), BF),
        pltpu.VMEM((N1, T, C), BF),
        pltpu.VMEM((NU, T, C), BF),
        pltpu.VMEM((NU, T, C), BF),
        pltpu.VMEM((NU, 2, T, C), BF),
        pltpu.VMEM((4, H, HID), BF),
        pltpu.VMEM((2 * HID, H), BF),
        pltpu.SemaphoreType.DMA, sems(2), sems(3), sems(3), sems(3),
        sems(NP), sems(NP), sems(2, ND), sems(2, ND), sems(NP), sems(NP), sems(NP, 2), sems(NP, 2),
        sems(2, R // RB), sems(2, R // RB),
        sems(NU), sems(NU), sems(NU), sems(NU), sems(NU), sems(NU), sems(NU), sems(NU),
        sems(N1, 2), sems(N1, 2), sems(N1), sems(N1),
        sems(NU, 2), sems(NU, 2), sems(NU, 2),
        sems(NU, 3), sems(NU, 3), sems(NU, 3),
    ]
    shapes = [((T, D), BF), ((1, D, HID), BF), ((1, D, HID), BF), ((1, HID, D), BF)]
    held = pl.pallas_call(
        body,
        out_shape=[pltpu.VMEM(*shape) for shape in shapes],
        in_specs=[anyspace, anyspace, vmem, vmem, anyspace, anyspace, anyspace],
        out_specs=[anyspace] * 4,
        scratch_shapes=scratch,
        compiler_params=pltpu.CompilerParams(
            collective_id=0, has_side_effects=True, vmem_limit_bytes=47 * 1024 * 1024
        ),
        cost_estimate=pl.CostEstimate(flops=6_000_000_000, bytes_accessed=20_000_000, transcendentals=100_000),
    )(tokens, cotangent, expert_ids.T, gate_scores.T, gate_weight, up_weight, down_weight)
    held = [pltpu.with_memory_space_constraint(h, pltpu.VMEM) for h in held]
    return tuple(
        pl.pallas_call(
            write_out,
            out_shape=[jax.ShapeDtypeStruct(*shape) for shape in shapes],
            in_specs=[anyspace] * 4,
            out_specs=[anyspace] * 4,
            scratch_shapes=[sems(4)],
            compiler_params=pltpu.CompilerParams(vmem_limit_bytes=2 * 1024 * 1024),
        )(*held)
    )


def solution(mesh):
    placed = (
        P("ep", None),
        P("ep", None),
        P("ep", None),
        P("ep", None),
        P("ep", None, "grp"),
        P("ep", None, "grp"),
        P("ep", "grp", None),
    )
    return jax.shard_map(
        per_device,
        mesh=mesh,
        in_specs=placed,
        out_specs=(P("ep", None), P("ep", None, "grp"), P("ep", None, "grp"), P("ep", "grp", None)),
        check_vma=False,
    )
```

```python
import functools

import jax
import jax.numpy as jnp
from jax import lax
from jax.experimental import pallas as pl
from jax.experimental.pallas import tpu as pltpu
from jax.sharding import PartitionSpec as P

BF = jnp.bfloat16
F32 = jnp.float32
MESH = pl.DeviceIdType.MESH

N = 16
SIDE = 4
T = 256
HID = 128
D = 7168
H = D // 2
W = 512
U = 128
C = 2 * U
NU = H // W
NA = H // C
NP = 5
ND = 6
R16 = N * 16
R8 = N * 8
R = R16 + R8
BLK = 48
OFFS = (
    (2, 2), (2, 3), (3, 2), (2, 1), (1, 2), (2, 0), (0, 2), (3, 1),
    (1, 3), (3, 3), (1, 1), (3, 0), (0, 3), (1, 0), (0, 1),
)
RB = 128
LAG = 4
GL = 3
N1 = 3


def mm(a, b, ca=1, cb=0):
    return lax.dot_general(a, b, (((ca,), (cb,)), ((), ())), preferred_element_type=F32)


def pack(dst, g):
    g16 = g[:R16].reshape(N, 16, C)
    dst[:, 0:16, :] = g16[:, :, :U].astype(BF)
    dst[:, 16:32, :] = g16[:, :, U:].astype(BF)
    g8 = g[R16:].reshape(N, 8, C)
    dst[:, 32:48, :] = jnp.concatenate([g8[:, :, :U], g8[:, :, U:]], axis=1).astype(BF)


def body(
    tok, cot, ids, gs, gw, uw, dw,
    o_tok, o_gate, o_up, o_down,
    tokv, tokd, pm, q16, q8a, q8b, scale, gate_col,
    send_a, send_d, recv_a, xm, wgu, wd, acc_gu, acc_h, accr_gu, accr_h, hid, g2,
    pk, rsb, send_c, recv_c, recv_i, zx, zy, zp, zr, fin, dwgu, dwd,
    tok_sem, tokd_sem, w_sem, ws_sem, wr_sem, as_sem, ar_sem, ds_a_sem, dr_a_sem, z1s_sem, z1r_sem, z2s_sem, z2r_sem,
    bs_sem, br_sem, ps_sem, pr_sem, cs_sem, cr_sem, xs_sem, xr_sem, gs_sem, gr_sem,
    is_sem, ir_sem, ts_sem, tr_sem,
    ol_sem, os_sem, or_sem, dl_sem, ds_sem, dr_sem,
):
    g = lax.axis_index("grp")
    e = lax.axis_index("ep")
    z, c = g // 2, g % 2
    x, y = e // SIDE, e % SIDE
    other = 1 - c
    npc = NP - c
    ndc = NA - 2 * npc
    za = z + 1 - 2 * (z % 2)
    zb = 3 - z
    zo = 3 - za
    sib = (2 * z + other, e)

    def first(i):
        return za + (zb - za) * ((i + c) % 2)

    def second(i):
        return zb + (za - zb) * ((i + c) % 2)

    def at_z(zz):
        return (2 * zz + c, e)

    def peer(k):
        dx, dy = OFFS[k]
        if dx != dy:
            dx, dy = dx * other + dy * c, dy * other + dx * c
        return ((x + dx) % SIDE) * SIDE + (y + dy) % SIDE

    def remote(src, dst, ss, rs, dev):
        return pltpu.make_async_remote_copy(
            src_ref=src, dst_ref=dst, send_sem=ss, recv_sem=rs, device_id=dev, device_id_type=MESH
        )

    def mult(v, m):
        return pl.multiple_of(v, m)

    bar = pltpu.get_barrier_semaphore()
    for k in range(N - 1):
        pl.semaphore_signal(bar, inc=1, device_id=(g, peer(k)), device_id_type=MESH)
    for dev in (at_z(za), at_z(zb), sib):
        pl.semaphore_signal(bar, inc=1, device_id=dev, device_id_type=MESH)

    def load(src):
        col = mult(c * H + (z % 2) * npc * C, C)
        return pltpu.make_async_copy(src.at[:, pl.ds(col, NP * C)], tokv, tok_sem)

    def load_d(a):
        col = mult(c * H + 2 * npc * C, C)
        return pltpu.make_async_copy((tok, cot)[a].at[:, pl.ds(col, ND * C)], tokd.at[a], tokd_sem.at[a])

    @pl.when(z < 2)
    def _():
        load(tok).start()

    @pl.when(z >= 2)
    def _():
        load(cot).start()

    for a in range(2):
        load_d(a).start()

    my_half = mult(c * H, H)
    own_w = [
        pltpu.make_async_copy(gw.at[0, pl.ds(my_half, H)], wgu.at[c], w_sem.at[0]),
        pltpu.make_async_copy(uw.at[0, pl.ds(my_half, H)], wgu.at[2 + c], w_sem.at[1]),
        pltpu.make_async_copy(
            dw.at[0, :, pl.ds(my_half, H)], wd.at[pl.ds(mult(c * HID, HID), HID)], w_sem.at[2]
        ),
    ]
    for cp in own_w:
        cp.start()

    def column(row):
        return jnp.transpose(jnp.broadcast_to(row, (128, T)))[:, 0:1]

    idf = ids[...].astype(F32)
    e_row = jnp.min(idf, axis=0, keepdims=True)
    e_col = column(e_row)
    sub = lax.broadcasted_iota(jnp.int32, (T, T), 0)
    lane = lax.broadcasted_iota(jnp.int32, (T, T), 1)
    before = jnp.where(sub < lane, jnp.where(e_col == e_row, 1.0, 0.0), 0.0)
    rank_row = jnp.sum(before, axis=0, keepdims=True)
    valid = e_row < N
    slot16 = jnp.where(valid & (rank_row < 16), e_row * 16 + rank_row, -1.0)
    slot8 = jnp.where(valid & (rank_row >= 16), e_row * 8 + (rank_row - 16), -1.0)

    def onehot(test):
        return jnp.where(test, 1.0, 0.0).astype(BF)

    subf = sub.astype(F32)
    pm[:R16, :] = onehot(subf == slot16)
    pm[R16:, :] = onehot(subf[:R8] == slot8)
    gate_row = jnp.sum(jnp.where(idf < N, gs[...], 0.0), axis=0, keepdims=True)
    gate_col[...] = column(gate_row)
    scale[...] = column(jnp.where(z < 2, jnp.ones_like(gate_row), gate_row))

    pl.semaphore_wait(bar, N - 1 + 3)

    their_half = mult(other * H, H)
    sib_w = [
        remote(gw.at[0, pl.ds(their_half, H)], wgu.at[c], ws_sem.at[0], wr_sem.at[0], sib),
        remote(uw.at[0, pl.ds(their_half, H)], wgu.at[2 + c], ws_sem.at[1], wr_sem.at[1], sib),
        remote(
            dw.at[0, :, pl.ds(their_half, H)],
            wd.at[pl.ds(mult(c * HID, HID), HID)],
            ws_sem.at[2], wr_sem.at[2], sib,
        ),
    ]

    def spread(buf, n, ss, rs):
        recv_a[n, e] = buf[e]
        for k in range(N - 1):
            dst = peer(k)
            remote(buf.at[dst], recv_a.at[n, e], ss, rs, (g, dst)).start()

    def part_of(owner, i):
        return (owner // 2) * NA + (owner % 2) * npc + i

    def dispatch(i, carry):
        src = tokv[:, pl.ds(mult(i * C, C), C)]
        src = (scale[...] * src.astype(F32)).astype(BF)
        pack(send_a.at[i], mm(pm[...], src))
        spread(send_a.at[i], part_of(z, i), as_sem.at[i], ar_sem.at[i])
        return carry

    def dispatch_d(d, carry=0):
        for a in range(2):
            src = tokd[a, :, pl.ds(mult(d * C, C), C)]
            if a == 1:
                src = (gate_col[...] * src.astype(F32)).astype(BF)
            pack(send_d.at[a, d], mm(pm[...], src))
            spread(send_d.at[a, d], a * NA + 2 * npc + d, ds_a_sem.at[a, d], dr_a_sem.at[a, d])
        return carry

    load(tok).wait()
    lax.fori_loop(0, npc, dispatch, 0)
    for cp in sib_w:
        cp.start()
    for a in range(2):
        load_d(a).wait()

    lanef = lane.astype(F32)
    q16[...] = onehot(lanef == column(slot16))
    late_a = jnp.where(valid & (rank_row >= 16), e_row * 16 + (rank_row - 16), -16.0)
    q8a[...] = onehot(lanef == column(late_a))
    q8b[...] = onehot(lanef == column(late_a + 8))
    acc_gu[...] = jnp.zeros_like(acc_gu)
    acc_h[...] = jnp.zeros_like(acc_h)

    def arrived(i):
        blocks = recv_a.at[part_of(z, i), pl.ds(0, N - 1)]
        return remote(blocks, blocks, as_sem.at[i], ar_sem.at[i], sib)

    def arrived_d(a, d):
        blocks = recv_a.at[a * NA + 2 * npc + d, pl.ds(0, N - 1)]
        return remote(blocks, blocks, ds_a_sem.at[a, d], dr_a_sem.at[a, d], sib)

    def unpack(a, m):
        r = recv_a[a * NA + m]
        late8 = r[:, 32:48, :].astype(F32)
        left, right = pl.ds(mult(m * C, U), U), pl.ds(mult(m * C + U, U), U)
        xm[a, :R16, left] = r[:, 0:16, :].reshape(R16, U)
        xm[a, R16:, left] = late8[:, 0:8, :].reshape(R8, U).astype(BF)
        xm[a, :R16, right] = r[:, 16:32, :].reshape(R16, U)
        xm[a, R16:, right] = late8[:, 8:16, :].reshape(R8, U).astype(BF)

    def multiply(a, m):
        cols = pl.ds(mult(m * C, C), C)
        if a == 0:
            w = jnp.concatenate([wgu[k, cols, :] for k in range(4)], axis=1)
            acc_gu[...] += mm(xm[0, :, cols], w)
        else:
            acc_h[...] += mm(xm[1, :, cols], wd[:, cols], 1, 1)

    def process_of(owner, i):
        a, m = owner // 2, (owner % 2) * npc + i
        unpack(a, m)

        @pl.when(a == 0)
        def _():
            multiply(0, m)

        @pl.when(a == 1)
        def _():
            multiply(1, m)

    def process_d(d):
        for a in range(2):
            arrived_d(a, d).wait_recv()
            unpack(a, 2 * npc + d)
            multiply(a, 2 * npc + d)

    def step1(i):
        blk = recv_a.at[part_of(z, i)]
        return remote(blk, blk, z1s_sem.at[i], z1r_sem.at[i], at_z(first(i)))

    def step2(i, fwd):
        blk = recv_a.at[part_of(first(i), i) if fwd else part_of(z, i)]
        return remote(blk, blk, z2s_sem.at[i, fwd], z2r_sem.at[i, fwd], at_z(second(i)))

    dispatch_d(0)

    def gather1(i, carry):
        arrived(i).wait_recv()
        step1(i).start()
        step2(i, 0).start()

        @pl.when(i + 1 < ndc)
        def _():
            dispatch_d(i + 1)

        return carry

    lax.fori_loop(0, npc, gather1, 0)
    lax.fori_loop(npc + 1, ndc, dispatch_d, 0)
    for k in range(3):
        own_w[k].wait()
        sib_w[k].wait_recv()

    def gather2(i, carry):
        step1(i).wait_recv()
        step2(i, 1).start()
        process_of(z, i)
        process_of(first(i), i)

        @pl.when((i >= 1) & (i < ndc + 1))
        def _():
            process_d(i - 1)

        return carry

    lax.fori_loop(0, npc, gather2, 0)

    def gather3(i, carry):
        @pl.when(i + npc - 1 < ndc)
        def _():
            process_d(i + npc - 1)

        step2(i, 0).wait_recv()
        process_of(second(i), i)
        step2(i, 1).wait_recv()
        process_of(zo, i)
        return carry

    lax.fori_loop(0, npc, gather3, 0)

    def swap(i):
        rows = pl.ds(mult(i * RB, RB), RB)
        return (
            remote(acc_gu.at[rows], accr_gu.at[rows], bs_sem.at[0, i], br_sem.at[0, i], sib),
            remote(acc_h.at[rows], accr_h.at[rows], bs_sem.at[1, i], br_sem.at[1, i], sib),
        )

    for i in range(R // RB):
        for cp in swap(i):
            cp.start()

    def act(i, carry):
        rows = pl.ds(mult(i * RB, RB), RB)
        for cp in swap(i):
            cp.wait_recv()
        gu = acc_gu[rows, :] + accr_gu[rows, :]
        gh = acc_h[rows, :] + accr_h[rows, :]
        gp, up = gu[:, : 2 * HID], gu[:, 2 * HID :]
        sg = jax.nn.sigmoid(gp)
        silu = gp * sg
        hid[rows, :] = (silu * up).astype(BF)
        g2[rows, : 2 * HID] = (gh * up * sg * (1.0 + gp * (1.0 - sg))).astype(BF)
        g2[rows, 2 * HID :] = (gh * silu).astype(BF)
        return carry

    lax.fori_loop(0, R // RB, act, 0)

    def half(j):
        b = ((z + 1) // 2) % 2
        return b + (z // 2 - b) * ((j + c) % 2)

    def pair(j):
        return remote(pk.at[j, 1 - half(j)], rsb.at[j], ps_sem.at[j], pr_sem.at[j], at_z(first(j)))

    def row_grad(j):
        cols = pl.ds(mult(j * W, W), W)
        w = jnp.concatenate([wgu[i, cols, :] for i in range(4)], axis=1)
        r = mm(g2[...], w, 1, 1)
        for h in range(2):
            pack(pk.at[j, h], r[:, h * C : (h + 1) * C])

    def early(j, carry):
        row_grad(j)
        for h in range(2):
            recv_i[j, h, e] = pk[j, h, e]
            for k in range(N - 1):
                dst = peer(k)
                remote(
                    pk.at[j, h, dst], recv_i.at[j, h, e], is_sem.at[j, h], ir_sem.at[j, h], (g, dst)
                ).start()
        return carry

    def summed(j, carry):
        row_grad(j)
        pair(j).start()
        return carry

    lax.fori_loop(0, 1, early, 0)
    lax.fori_loop(N1, NU, summed, 0)
    lax.fori_loop(1, N1, early, 0)

    def back(j, carry):
        pair(j).wait_recv()
        send_c[j] = (pk[j, half(j)].astype(F32) + rsb[j].astype(F32)).astype(BF)
        recv_c[j, e] = send_c[j, e]
        for k in range(N - 1):
            dst = peer(k)
            remote(send_c.at[j, dst], recv_c.at[j, e], cs_sem.at[j], cr_sem.at[j], (g, dst)).start()
        return carry

    lax.fori_loop(N1, NU, back, 0)

    def early_all(j, h):
        blocks = recv_i.at[j, h, pl.ds(0, N - 1)]
        return remote(blocks, blocks, is_sem.at[j, h], ir_sem.at[j, h], sib)

    def give(j):
        return remote(zx.at[j], zy.at[j], ts_sem.at[j], tr_sem.at[j], at_z(first(j)))

    def cross(j):
        return remote(zp.at[j], zr.at[j], xs_sem.at[j], xr_sem.at[j], at_z(second(j)))

    def whole(j):
        blk = fin.at[j, half(j)]
        return remote(blk, blk, gs_sem.at[j], gr_sem.at[j], at_z(first(j)))

    def out_cols(j, p):
        return pl.ds(mult(c * H + j * W + p * C, C), C)

    def out_local(j, p):
        return pltpu.make_async_copy(fin.at[j, p], o_tok.at[:, out_cols(j, p)], ol_sem.at[j, p])

    def out_sib(j, p):
        return remote(fin.at[j, p], o_tok.at[:, out_cols(j, p)], os_sem.at[j, p], or_sem.at[j, p], sib)

    def grads_out(j):
        rows = pl.ds(mult(j * W, W), W)
        orow = pl.ds(mult(c * H + j * W, W), W)
        local, far = [], []
        for i, out in enumerate((o_gate, o_up)):
            local.append(pltpu.make_async_copy(dwgu.at[2 * i + c, rows], out.at[0, orow], dl_sem.at[j, i]))
            far.append(remote(dwgu.at[2 * i + other, rows], out.at[0, orow], ds_sem.at[j, i], dr_sem.at[j, i], sib))
        mine, yours = pl.ds(mult(c * HID, HID), HID), pl.ds(mult(other * HID, HID), HID)
        local.append(pltpu.make_async_copy(dwd.at[mine, rows], o_down.at[0, :, orow], dl_sem.at[j, 2]))
        far.append(remote(dwd.at[yours, rows], o_down.at[0, :, orow], ds_sem.at[j, 2], dr_sem.at[j, 2], sib))
        return local, far

    def scatter(r):
        r8 = r[:, 32:48, :].reshape(R16, U)
        parts = []
        for p in range(2):
            r16 = r[:, 16 * p : 16 * p + 16, :].reshape(R16, U)
            parts.append((mm(q16[...], r16) + mm((q8a, q8b)[p][...], r8)).astype(BF))
        return jnp.concatenate(parts, axis=1)

    def crossed(j):
        cross(j).wait_recv()
        fin[j, half(j)] = (zp[j].astype(F32) + zr[j].astype(F32)).astype(BF)
        whole(j).start()

    def finished(j):
        whole(j).wait_recv()
        for p in range(2):
            out_local(j, p).start()
            out_sib(j, p).start()

    def pipe(t, carry):
        @pl.when(t < N1)
        def _():
            for h in range(2):
                early_all(t, h).wait_recv()
            zx[t] = scatter(recv_i[t, 1 - half(t)])
            give(t).start()
            zp[t] = scatter(recv_i[t, half(t)])

        @pl.when((t >= N1) & (t < NU))
        def _():
            blocks = recv_c.at[t, pl.ds(0, N - 1)]
            remote(blocks, blocks, cs_sem.at[t], cr_sem.at[t], sib).wait_recv()
            zp[t] = scatter(recv_c[t])
            cross(t).start()

        @pl.when((t >= GL) & (t < N1 + GL))
        def _():
            j = t - GL
            give(j).wait_recv()
            zp[j] = (zp[j].astype(F32) + zy[j].astype(F32)).astype(BF)
            cross(j).start()

        @pl.when((t >= GL + LAG) & (t < N1 + GL + LAG))
        def _():
            crossed(t - GL - LAG)

        @pl.when((t >= N1 + LAG) & (t < NU + LAG))
        def _():
            crossed(t - LAG)

        @pl.when((t >= GL + 2 * LAG) & (t < N1 + GL + 2 * LAG))
        def _():
            finished(t - GL - 2 * LAG)

        @pl.when(t >= N1 + 2 * LAG)
        def _():
            finished(t - 2 * LAG)

        @pl.when(t < NU)
        def _():
            cols = pl.ds(mult(t * W, W), W)
            d1 = mm(xm[0, :, cols], g2[...], 0, 0)
            for i in range(4):
                dwgu[i, cols, :] = d1[:, i * HID : (i + 1) * HID].astype(BF)
            dwd[:, cols] = mm(hid[...], xm[1, :, cols], 0, 0).astype(BF)
            local, far = grads_out(t)
            for cp in local + far:
                cp.start()

        return carry

    lax.fori_loop(0, NU + 2 * LAG, pipe, 0)

    for i in range(3):
        sib_w[i].wait_send()
        for cp in swap(i):
            cp.wait_send()

    def drain_a(i, carry):
        arrived(i).wait_send()
        step1(i).wait_send()
        step2(i, 0).wait_send()
        step2(i, 1).wait_send()
        return carry

    lax.fori_loop(0, npc, drain_a, 0)

    def drain_d(d, carry):
        for a in range(2):
            arrived_d(a, d).wait_send()
        return carry

    lax.fori_loop(0, ndc, drain_d, 0)

    for j in range(N1):
        give(j).wait_send()
        for h in range(2):
            early_all(j, h).wait_send()

    def drain_c(j, carry):
        blocks = send_c.at[j, pl.ds(0, N - 1)]
        remote(blocks, blocks, cs_sem.at[j], cr_sem.at[j], sib).wait_send()
        pair(j).wait_send()
        return carry

    lax.fori_loop(N1, NU, drain_c, 0)

    def drain(j, carry):
        for cp in (cross(j), whole(j)):
            cp.wait_send()
        for p in range(2):
            out_local(j, p).wait()
            out_sib(j, p).wait()
        local, far = grads_out(j)
        for cp in local + far:
            cp.wait()
        return carry

    lax.fori_loop(0, NU, drain, 0)


def write_out(*refs):
    sem = refs[8]
    copies = [pltpu.make_async_copy(refs[i], refs[4 + i], sem.at[i]) for i in range(4)]
    for cp in copies:
        cp.start()
    for cp in copies:
        cp.wait()


def per_device(tokens, cotangent, expert_ids, gate_scores, gate_weight, up_weight, down_weight):
    def sems(*shape):
        return pltpu.SemaphoreType.DMA(shape)

    anyspace = pl.BlockSpec(memory_space=pl.ANY)
    vmem = pl.BlockSpec(memory_space=pltpu.VMEM)
    scratch = [
        pltpu.VMEM((T, NP * C), BF),
        pltpu.VMEM((2, T, ND * C), BF),
        pltpu.VMEM((R, T), BF),
        pltpu.VMEM((T, R16), BF),
        pltpu.VMEM((T, R16), BF),
        pltpu.VMEM((T, R16), BF),
        pltpu.VMEM((T, 1), F32),
        pltpu.VMEM((T, 1), F32),
        pltpu.VMEM((NP, N, BLK, U), BF),
        pltpu.VMEM((2, ND, N, BLK, U), BF),
        pltpu.VMEM((2 * NA, N, BLK, U), BF),
        pltpu.VMEM((2, R, H), BF),
        pltpu.VMEM((4, H, HID), BF),
        pltpu.VMEM((2 * HID, H), BF),
        pltpu.VMEM((R, 4 * HID), F32),
        pltpu.VMEM((R, 2 * HID), F32),
        pltpu.VMEM((R, 4 * HID), F32),
        pltpu.VMEM((R, 2 * HID), F32),
        pltpu.VMEM((R, 2 * HID), BF),
        pltpu.VMEM((R, 4 * HID), BF),
        pltpu.VMEM((NU, 2, N, BLK, U), BF),
        pltpu.VMEM((NU, N, BLK, U), BF),
        pltpu.VMEM((NU, N, BLK, U), BF),
        pltpu.VMEM((NU, N, BLK, U), BF),
        pltpu.VMEM((N1, 2, N, BLK, U), BF),
        pltpu.VMEM((N1, T, C), BF),
        pltpu.VMEM((N1, T, C), BF),
        pltpu.VMEM((NU, T, C), BF),
        pltpu.VMEM((NU, T, C), BF),
        pltpu.VMEM((NU, 2, T, C), BF),
        pltpu.VMEM((4, H, HID), BF),
        pltpu.VMEM((2 * HID, H), BF),
        pltpu.SemaphoreType.DMA, sems(2), sems(3), sems(3), sems(3),
        sems(NP), sems(NP), sems(2, ND), sems(2, ND), sems(NP), sems(NP), sems(NP, 2), sems(NP, 2),
        sems(2, R // RB), sems(2, R // RB),
        sems(NU), sems(NU), sems(NU), sems(NU), sems(NU), sems(NU), sems(NU), sems(NU),
        sems(N1, 2), sems(N1, 2), sems(N1), sems(N1),
        sems(NU, 2), sems(NU, 2), sems(NU, 2),
        sems(NU, 3), sems(NU, 3), sems(NU, 3),
    ]
    shapes = [((T, D), BF), ((1, D, HID), BF), ((1, D, HID), BF), ((1, HID, D), BF)]
    held = pl.pallas_call(
        body,
        out_shape=[pltpu.VMEM(*shape) for shape in shapes],
        in_specs=[anyspace, anyspace, vmem, vmem, anyspace, anyspace, anyspace],
        out_specs=[anyspace] * 4,
        scratch_shapes=scratch,
        compiler_params=pltpu.CompilerParams(
            collective_id=0, has_side_effects=True, vmem_limit_bytes=47 * 1024 * 1024
        ),
        cost_estimate=pl.CostEstimate(flops=6_000_000_000, bytes_accessed=20_000_000, transcendentals=100_000),
    )(tokens, cotangent, expert_ids.T, gate_scores.T, gate_weight, up_weight, down_weight)
    held = [pltpu.with_memory_space_constraint(h, pltpu.VMEM) for h in held]
    return tuple(
        pl.pallas_call(
            write_out,
            out_shape=[jax.ShapeDtypeStruct(*shape) for shape in shapes],
            in_specs=[anyspace] * 4,
            out_specs=[anyspace] * 4,
            scratch_shapes=[sems(4)],
            compiler_params=pltpu.CompilerParams(vmem_limit_bytes=2 * 1024 * 1024),
        )(*held)
    )


def solution(mesh):
    placed = (
        P("ep", None),
        P("ep", None),
        P("ep", None),
        P("ep", None),
        P("ep", None, "grp"),
        P("ep", None, "grp"),
        P("ep", "grp", None),
    )
    return jax.shard_map(
        per_device,
        mesh=mesh,
        in_specs=placed,
        out_specs=(P("ep", None), P("ep", None, "grp"), P("ep", None, "grp"), P("ep", "grp", None)),
        check_vma=False,
    )
```
